256 devices in a mesh: seq: 16 (over y, x), mem: 16 (over z, core).
Axes of the slice: x: 4, y: 4, z: 8, core: 2. Of those that a mesh axis runs over, the one named last changes fastest.
Arguments:
- hidden: bfloat16 [65536, 2048], P(('seq', 'mem')), may hold values from -6 to 6
- routes: int32 [65536, 2], P(('seq', 'mem')), may hold values from 0 to 15, all different within a row; in each aligned block of 256 rows (0 to 255, 256 to 511, ...) at most 64 rows name the same one
- gate_levels: int32 [65536, 2], P(('seq', 'mem')), may hold values from 1 to 255
- query_weight: bfloat16 [2048, 1024], P('seq'), may hold values from -0.125 to 0.125
- key_weight: bfloat16 [16, 2048, 1024], P('mem', 'seq'), may hold values from -0.125 to 0.125
- value_weight: bfloat16 [16, 2048, 1024], P('mem', 'seq'), may hold values from -0.125 to 0.125
Outputs:
- mixed: bfloat16 [65536, 1024], P(('seq', 'mem'))
The draws below stay inside these ranges and needn't reach their ends.
Inputs may be any that keep to these rules, and one draw needn't show every extreme that they name: `routes`: the two memories of a row differ. In the rows of one device no memory is named by more than 64 rows, a bound that some block reaches.
All inputs are finite; a program needn't handle non-finite values.
Results may differ from the reference program's by a relative error of at most 0.01.
Values may be sent and summed in bfloat16 or wider, within the bound.
A program may use at most 128 MiB of HBM per device.

```python
import math
import jax
import jax.numpy as jnp
import numpy as np
from jax import lax

D = 2048
HEADS = 8
DK = 128
TOK_DEV = 256
BLOCK = 512
CAP = 64
HD = 1024
EXPERTS = 16
TOKENS = 65536


def plant(array, own_key, low, largest):
    dims = array.shape
    place = [jax.random.randint(jax.random.fold_in(own_key, axis), (), 0, dims[axis]) for axis in range(len(dims))]
    array = array.at[tuple(place)].set(low)
    longest = dims.index(max(dims))
    place[longest] = (place[longest] + 1) % dims[longest]
    return array.at[tuple(place)].set(largest)


def shard_levels(rng, dims, cuts, low, top_value):
    gain = 1.0
    for dim, parts in cuts:
        draws = jax.random.uniform(jax.random.fold_in(jax.random.fold_in(rng, 6), dim), (parts,), jnp.float32, low / len(cuts), top_value / len(cuts))
        gain = gain * jnp.repeat(jnp.exp(draws), dims[dim] // parts).reshape((-1,) + (1,) * (len(dims) - 1 - dim))
    return gain


def deal_out(key, own, number, rows, number_of, top, limit, lean):
    order = jax.random.permutation(key, number_of)
    crowded, usual = shares(number_of, rows * top, limit, lean, True), shares(number_of, rows * top, limit, lean, False)
    places = jnp.arange(number_of)

    def named(sizes, turn):
        used = int((sizes > 0).sum())
        fixed = max(1, used // 4)
        passed = fixed + (places - fixed + turn * (used - fixed)) % max(1, number_of - fixed)
        return jnp.zeros((number_of,), jnp.int32).at[order[jnp.where(places < fixed, places, passed)]].set(jnp.asarray(sizes, jnp.int32))

    sizes = jnp.where(number % 4 == 0, named(crowded, number // 4), named(usual, number - number // 4 - 1))
    mixed = jax.random.permutation(jax.random.fold_in(own, 3), number_of)
    donor, taker = mixed[0:number_of // 2 * 2:2], mixed[1:number_of // 2 * 2:2]
    margin = jnp.minimum(sizes[donor] - 1, limit - sizes[taker]) // 2
    margin = jnp.where((donor == order[0]) | (taker == order[0]) | (sizes[taker] == 0), 0, jnp.maximum(margin, 0))
    passed = jax.random.randint(jax.random.fold_in(own, 4), (number_of // 2,), 0, 1 << 20) % (margin + 1)
    sizes = sizes.at[donor].add(-passed).at[taker].add(passed)
    members = jnp.searchsorted(jnp.cumsum(sizes), jnp.arange(rows * top), side="right").astype(jnp.int32)
    grid = members.reshape(top, rows).T
    grid = grid[jax.random.permutation(jax.random.fold_in(own, 1), rows)]
    turn = jax.random.randint(jax.random.fold_in(own, 2), (rows, 1), 0, top)
    return jnp.take_along_axis(grid, (jnp.arange(top)[None, :] + turn) % top, axis=1)


def shares(amount, total, reach, lean, full):
    loads = [(1 << 20) // math.isqrt(rank ** lean) + 1 for rank in range(1, amount + 1)]
    largest = reach if full else min(reach, max(-(-total // amount), total * loads[0] // sum(loads)))
    least = 1 if total - largest >= amount - 1 else 0
    given, surplus = [largest] + [least] * (amount - 1), total - largest - least * (amount - 1)
    while surplus > 0:
        candidates = [i for i in range(1, amount) if given[i] < largest] or [i for i in range(1, amount) if given[i] < reach]
        whole, budget = sum([loads[i] for i in candidates]), surplus
        for i in candidates:
            extra = min(reach - given[i], max(1, budget * loads[i] // whole), surplus)
            given[i] = given[i] + extra
            surplus = surplus - extra
    return np.array(given)


def bell_draw(key, shape, scale, bound, shards=(), kind=jnp.bfloat16):
    loudness = shard_levels(key, shape, shards, -0.22, 0.18) if shards else 1.0
    result = jax.random.normal(key, shape, jnp.float32) * scale * loudness
    return jnp.minimum(jnp.maximum(result, -bound), bound).astype(kind)


def setup_inputs(seed: int = 0) -> dict:
    key_list = jax.random.split(jax.random.key(seed), 7)
    hidden = bell_draw(key_list[0], (TOKENS, D), 1.0, 6.0, ((0, 256),))
    routes_keys = jax.random.split(jax.random.fold_in(key_list[1], 1), TOKENS // TOK_DEV)
    routes_turns = jax.random.permutation(jax.random.fold_in(key_list[1], 3), TOKENS // TOK_DEV)
    routes = jax.vmap(lambda own, number: deal_out(jax.random.fold_in(key_list[1], 2), own, number, TOK_DEV, EXPERTS, 2, CAP, 2))(routes_keys, routes_turns).reshape((TOKENS, 2))
    gate_levels = plant(jax.random.randint(key_list[2], (TOKENS, 2), 1, 256), jax.random.fold_in(key_list[2], 1), 1, 255).astype(jnp.int32)
    query_weight = bell_draw(key_list[3], (D, HD), D ** -0.5, 0.125, ((0, 16),))
    key_weight = bell_draw(key_list[4], (EXPERTS, D, HD), D ** -0.5, 0.125, ((0, 16), (1, 16)))
    value_weight = bell_draw(key_list[5], (EXPERTS, D, HD), D ** -0.5, 0.125, ((0, 16), (1, 16)))
    return dict(hidden=hidden, routes=routes, gate_levels=gate_levels, query_weight=query_weight, key_weight=key_weight, value_weight=value_weight)


def reference(hidden, routes, gate_levels, query_weight, key_weight, value_weight):
    tokens = hidden.shape[0]
    width = query_weight.shape[1]
    highest = lax.Precision.HIGHEST
    queries = jnp.dot(hidden, query_weight, preferred_element_type=jnp.float32).astype(jnp.bfloat16)
    levels = gate_levels.astype(jnp.float32)
    gates = levels / lax.optimization_barrier(jnp.sum(levels, axis=1, keepdims=True))
    padded = tokens // TOK_DEV * CAP
    blocks = padded // BLOCK
    order = jnp.arange(tokens, dtype=jnp.int32)
    rowids = jnp.arange(BLOCK, dtype=jnp.int32)
    causal = (rowids[:, None] >= rowids[None, :]).astype(jnp.float32)

    def step(state, inputs):
        q_block, k_block, v_block = inputs
        scores = jnp.einsum('qhd,khd->hqk', q_block, k_block, precision=highest) * causal[None]
        local = jnp.einsum('hqk,khd->qhd', scores, v_block, precision=highest)
        carried = jnp.einsum('qhd,hde->qhe', q_block, state, precision=highest)
        state = state + jnp.einsum('khd,khe->hde', k_block, v_block, precision=highest)
        return (state, local + carried)

    def memory(expert, total):
        hit = routes == expert
        flag = jnp.any(hit, axis=1)
        keyed = jnp.where(flag, order, order + tokens)
        picked = jnp.argsort(keyed)[:padded].astype(jnp.int32)
        valid = jnp.arange(padded, dtype=jnp.int32) < jnp.sum(flag.astype(jnp.int32))
        chosen = jnp.where(valid[:, None], jnp.take(hidden, picked, axis=0), jnp.zeros((), hidden.dtype))
        w_key = lax.dynamic_index_in_dim(key_weight, expert, 0, keepdims=False)
        w_value = lax.dynamic_index_in_dim(value_weight, expert, 0, keepdims=False)
        keys = jnp.dot(chosen, w_key, preferred_element_type=jnp.float32).astype(jnp.bfloat16)
        values = jnp.dot(chosen, w_value, preferred_element_type=jnp.float32).astype(jnp.bfloat16)
        q_sel = jnp.where(valid[:, None], jnp.take(queries, picked, axis=0), jnp.zeros((), queries.dtype))
        shape4 = (blocks, BLOCK, HEADS, DK)
        q_four = q_sel.astype(jnp.float32).reshape(shape4)
        k_four = keys.astype(jnp.float32).reshape(shape4)
        v_four = values.astype(jnp.float32).reshape(shape4)
        start = jnp.zeros((HEADS, DK, DK), jnp.float32)
        _, reads = lax.scan(step, start, (q_four, k_four, v_four))
        scale = lax.rsqrt(lax.optimization_barrier(jnp.mean(reads * reads, axis=-1, keepdims=True)) + 1e-06)
        normed = (reads * scale).astype(jnp.bfloat16).astype(jnp.float32).reshape(padded, width)
        weight = lax.optimization_barrier(jnp.sum(jnp.where(hit, gates, jnp.zeros((), jnp.float32)), axis=1))
        weight = jnp.where(valid, jnp.take(weight, picked, axis=0), jnp.zeros((), jnp.float32))
        return total.at[picked].add(weight[:, None] * normed)
    total = lax.fori_loop(0, EXPERTS, memory, jnp.zeros((tokens, width), jnp.float32))
    return total.astype(jnp.bfloat16)
```

```python
import jax
import jax.numpy as jnp
from jax import lax
from jax.experimental import pallas as pl
from jax.experimental.pallas import tpu as pltpu
from jax.sharding import PartitionSpec as P

D = 2048
HD = 1024
HEADS = 8
DK = 128
TOK = 256
CAP = 64
MEMS = 16
SIDE = 4
RING = 8
ROWS = MEMS * CAP
BLOCK = 256
BF16 = jnp.bfloat16
F32 = jnp.float32
MESH = pl.DeviceIdType.MESH


def tiles(total, width, body):
    @pl.loop(0, total // width)
    def _(step):
        body(pl.ds(pl.multiple_of(step * width, width), width))


def weight_stream(whole, own, base, n, x_first, y, x, send_sems, recv_sems):
    f = x_first * x + (1 - x_first) * y
    g = x_first * y + (1 - x_first) * x

    def place(i, j):
        a, b = lax.rem(f + i + SIDE, SIDE), lax.rem(g + j + SIDE, SIDE)
        return x_first * (b * SIDE + a) + (1 - x_first) * (a * SIDE + b)

    def piece(i, j, part=None):
        start, rows = base, n
        if part is not None:
            start, rows = base + part * (n // 2), n // 2
        return whole.at[place(i, j), pl.ds(start, rows), :]

    def send(number, src, dst, i, j):
        return pltpu.make_async_remote_copy(
            src_ref=src,
            dst_ref=dst,
            send_sem=send_sems.at[number],
            recv_sem=recv_sems.at[number],
            device_id={"seq": place(i, j)},
            device_id_type=MESH,
        )

    def relay(number, i, j, part, di, dj):
        return send(number, piece(i, j, part), piece(i, j, part), di, dj)

    first = [send(c, own, piece(0, 0), *to) for c, to in enumerate(((1, 0), (-1, 0), (0, 1), (0, -1)))]
    copies = first + [
        relay(4, -1, 0, 0, 1, 0),
        relay(5, 1, 0, 1, -1, 0),
        relay(6, 0, -1, 0, 0, 1),
        relay(7, 0, 1, 1, 0, -1),
        relay(8, -1, 0, None, 0, 1),
        relay(9, -1, 0, None, 0, -1),
        relay(10, 1, 0, None, 0, 1),
        relay(11, 1, 0, None, 0, -1),
        relay(12, 2, 0, None, 0, 1),
        relay(13, 2, 0, None, 0, -1),
        relay(14, -1, -1, 0, 0, 1),
        relay(15, -1, 1, 1, 0, -1),
        relay(16, 1, -1, 0, 0, 1),
        relay(17, 1, 1, 1, 0, -1),
        relay(18, 2, -1, 0, 0, 1),
        relay(19, 2, 1, 1, 0, -1),
    ]
    return copies


def kernel(
    hid, routes, levels, qw, kw, vw, out,
    raw, tab, rows_in, stage, sib_stage, wq, wk, wv, q, k, v, xs,
    total, entering, part_states, s_send, s_recv, reads, normed,
    ret, own_ret, gates, own_gates, part_out, part_in,
    w_send, w_recv, raw_sems, tab_sems, set_send, set_recv, sib_send, local_sems, swap_sems,
    state_sems, ret_send, ret_recv, own_ret_sems, part_sems,
):
    me, group = lax.axis_index("mem"), lax.axis_index("seq")
    z, core = me // 2, me % 2
    y, x = group // SIDE, group % SIDE

    def mem(chip, c):
        return lax.rem(chip + RING, RING) * 2 + c

    def rcopy(src, dst, send_sem, recv_sem, device):
        return pltpu.make_async_remote_copy(
            src_ref=src, dst_ref=dst, send_sem=send_sem, recv_sem=recv_sem, device_id=device, device_id_type=MESH
        )

    def block(ref, source, rows=CAP):
        return ref.at[pl.ds(pl.multiple_of(source * rows, rows), rows), :]

    sent = []

    def go(copy):
        copy.start()
        sent.append(copy)
        return copy

    other = mem(z, 1 - core)
    barrier = pltpu.get_barrier_semaphore()
    peers = [{"mem": other}]
    peers += [{"mem": mem(z + d, c)} for d in (-3, -2, -1, 1, 2, 3) for c in (0, 1)]
    for dx, dy in ((1, 0), (3, 0), (0, 1), (0, 3)):
        peers.append({"seq": lax.rem(y + dy, SIDE) * SIDE + lax.rem(x + dx, SIDE)})
    for peer in peers:
        pl.semaphore_signal(barrier, inc=1, device_id=peer, device_id_type=MESH)

    mine = [
        pltpu.make_async_copy(hid, raw.at[2], local_sems.at[0]),
        pltpu.make_async_copy(kw.at[0], wk.at[group], local_sems.at[1]),
        pltpu.make_async_copy(vw.at[0], wv.at[group], local_sems.at[2]),
    ]
    half = pl.multiple_of(core * CAP, CAP)
    mine.append(
        pltpu.make_async_copy(qw.at[pl.ds(half, CAP), :], wq.at[group, pl.ds(half, CAP), :], local_sems.at[3])
    )
    for copy in mine:
        copy.start()
    ids = lax.broadcasted_iota(jnp.int32, (MEMS, TOK), 0)
    hit0, hit1 = routes[0:1, :] == ids, routes[1:2, :] == ids
    earlier = lax.broadcasted_iota(jnp.int32, (TOK, TOK), 0) < lax.broadcasted_iota(jnp.int32, (TOK, TOK), 1)
    hits = jnp.where(hit0 | hit1, 1.0, 0.0)
    place = jnp.dot(hits.astype(BF16), jnp.where(earlier, 1.0, 0.0).astype(BF16), preferred_element_type=F32)
    lev0, lev1 = levels[0:1, :].astype(F32), levels[1:2, :].astype(F32)
    both = lev0 + lev1
    tab[2, 0:MEMS, :] = jnp.where(hits > 0, place, -1.0)
    tab[2, MEMS : 2 * MEMS, :] = jnp.where(hit0, lev0 / both, 0.0) + jnp.where(hit1, lev1 / both, 0.0)

    pl.semaphore_wait(barrier, len(peers))

    raws, tabs = [], []
    for side, step in ((0, 1), (1, -1)):
        to = {"mem": mem(z + step, core)}
        tabs.append(go(rcopy(tab.at[2], tab.at[side], tab_sems.at[0, side], tab_sems.at[1, side], to)))
        raws.append(go(rcopy(hid, raw.at[side], raw_sems.at[0, side], raw_sems.at[1, side], to)))
    streams = [
        weight_stream(wk, kw.at[0], 0, 128, 1, y, x, w_send.at[0], w_recv.at[0]),
        weight_stream(wv, vw.at[0], 0, 128, 0, y, x, w_send.at[1], w_recv.at[1]),
        weight_stream(wq, qw.at[pl.ds(half, CAP), :], half, CAP, 1 - core, y, x, w_send.at[2], w_recv.at[2]),
    ]

    def start(*numbers):
        for number in numbers:
            for copies in streams:
                go(copies[number])

    def arrive(*numbers):
        for number in numbers:
            for copies in streams:
                copies[number].wait_recv()

    start(0, 1, 2, 3)

    slot = lax.broadcasted_iota(jnp.int32, (CAP, TOK), 0).astype(F32)

    def matches(index, mems):
        return [slot == tab[index, pl.ds(e, 1), :] for e in mems]

    def pack(index, mems, dest):
        ones = [jnp.where(m, 1.0, 0.0).astype(BF16) for m in matches(index, mems)]
        chosen = jnp.concatenate(ones, axis=0)

        def body(cols):
            dest[:, cols] = jnp.dot(chosen, raw[index, :, cols], preferred_element_type=F32).astype(BF16)

        tiles(D, 256, body)

    def mixing(index, mems, dest, width):
        parts = [
            jnp.where(m, tab[index, pl.ds(MEMS + e, 1), :], 0.0) for m, e in zip(matches(index, mems), mems)
        ]
        if width > len(mems) * CAP:
            parts.append(jnp.zeros((width - len(mems) * CAP, TOK), F32))
        weights = jnp.concatenate(parts, axis=0).T
        high = weights.astype(BF16)
        dest[0] = high
        dest[1] = (weights - high.astype(F32)).astype(BF16)

    def served(side):
        step = 1 - 2 * side
        return [
            me, other,
            mem(z + step, 0), mem(z + step, 1),
            mem(z + 2 * step, 0), mem(z + 2 * step, 1),
            mem(z + 3 * step, side),
        ]

    for copy in mine:
        copy.wait()
    pack(2, [me, other], sib_stage)
    block(rows_in, me)[...] = sib_stage[0:CAP, :]
    go(rcopy(sib_stage.at[pl.ds(CAP, CAP), :], block(rows_in, me), sib_send, set_recv.at[me], {"mem": other}))
    mixing(2, [me, other], own_gates, 2 * CAP)

    arrive(0, 1, 2, 3)
    start(8, 9, 10, 11, 4, 5, 6, 7)

    for side in (0, 1):
        origin = mem(z - 1 + 2 * side, core)
        mems = served(side)
        tabs[side].wait_recv()
        raws[side].wait_recv()
        pack(side, mems, stage.at[side])
        for number in (6, 4, 5, 2, 3, 1):
            go(
                rcopy(
                    stage.at[side, pl.ds(number * CAP, CAP), :],
                    block(rows_in, origin),
                    set_send.at[side, number],
                    set_recv.at[origin],
                    {"mem": mems[number]},
                )
            )
        block(rows_in, origin)[...] = stage[side, 0:CAP, :]

    arrive(4, 5, 8, 9, 10, 11)
    start(12, 13, 14, 15, 16, 17)
    for side in (0, 1):
        mixing(side, served(side), gates.at[side], 8 * CAP)
        ret[side, 7 * CAP : 8 * CAP, :] = jnp.zeros((CAP, HD), BF16)
    arrive(12, 13)
    start(18, 19)
    arrive(6, 7, 14, 15, 16, 17, 18, 19)
    swap = go(
        rcopy(
            wq.at[:, pl.ds(half, CAP), :],
            wq.at[:, pl.ds(half, CAP), :],
            swap_sems.at[0],
            swap_sems.at[1],
            {"mem": other},
        )
    )

    def take(sources, wait):
        for n, source in enumerate(sources):
            if wait[n]:
                rcopy(
                    block(rows_in, source), block(rows_in, source), sib_send, set_recv.at[source], {"mem": other}
                ).wait_recv()
            xs[n * CAP : (n + 1) * CAP, :] = block(rows_in, source)[...]

    def project(sources, weight, dest):
        many = len(sources) * CAP

        def body(cols):
            w = weight[:, :, cols].reshape(D, 256)
            result = jnp.dot(xs[0:many, :], w, preferred_element_type=F32).astype(BF16)
            for n, source in enumerate(sources):
                dest[pl.ds(pl.multiple_of(source * CAP, CAP), CAP), cols] = result[n * CAP : (n + 1) * CAP]

        tiles(HD, 256, body)

    near = [me, other] + [mem(z + d, c) for d in (-1, 1) for c in (core, 1 - core)]
    take(near, [False, True, False, True, False, True])
    project(near, wk, k)
    project(near, wv, v)
    swap.wait_recv()
    project(near, wq, q)
    middle = [mem(z + d, c) for d in (-2, 2) for c in (0, 1)]
    take(middle, [True] * 4)
    project(middle, wk, k)
    project(middle, wv, v)
    project(middle, wq, q)
    far = [mem(z + d, c) for d in (-3, 3, 4) for c in (0, 1)]
    take(far, [True] * 6)
    project(far, wk, k)
    project(far, wv, v)

    @pl.loop(0, HEADS)
    def _(h):
        cols = pl.ds(pl.multiple_of(h * DK, DK), DK)
        running = jnp.zeros((DK, DK), F32)
        for b in range(ROWS // BLOCK):
            if b:
                part_states[b - 1, cols, :] = running.astype(BF16)
            rows = slice(b * BLOCK, (b + 1) * BLOCK)
            running = running + lax.dot_general(
                k[rows, cols], v[rows, cols], (((0,), (0,)), ((), ())), preferred_element_type=F32
            )
        total[cols, :] = running

    causal = lax.broadcasted_iota(jnp.int32, (BLOCK, BLOCK), 0) >= lax.broadcasted_iota(
        jnp.int32, (BLOCK, BLOCK), 1
    )

    def attend(low, high):
        @pl.loop(low, high)
        def _(h):
            cols = pl.ds(pl.multiple_of(h * DK, DK), DK)
            for b in range(ROWS // BLOCK):
                rows = slice(b * BLOCK, (b + 1) * BLOCK)
                queries = q[rows, cols]
                scores = lax.dot_general(
                    queries, k[rows, cols], (((1,), (1,)), ((), ())), preferred_element_type=F32
                )
                scores = jnp.where(causal, scores, 0.0).astype(BF16)
                read = jnp.dot(scores, v[rows, cols], preferred_element_type=F32)
                if b:
                    read = read + jnp.dot(queries, part_states[b - 1, cols, :], preferred_element_type=F32)
                reads[rows, cols] = read

    partners = [
        (y * SIDE + (x + 1 - 2 * (x % 2)), x % 2),
        (y * SIDE + (SIDE - 1 - x), x // 2),
        ((y + 1 - 2 * (y % 2)) * SIDE + x, y % 2),
        ((SIDE - 1 - y) * SIDE + x, y // 2),
    ]
    entering[...] = jnp.zeros_like(entering)
    for step, (partner, later) in enumerate(partners):
        s_send[step] = total[...].astype(BF16)
        copy = go(
            rcopy(
                s_send.at[step], s_recv.at[step], state_sems.at[0, step], state_sems.at[1, step], {"seq": partner}
            )
        )
        if step == 0:
            project(far, wq, q)
            attend(0, 2)
        else:
            attend(2 * step, 2 * step + 2)
        copy.wait_recv()
        theirs = s_recv[step].astype(F32)
        entering[...] += theirs * later.astype(F32)
        if step < 3:
            total[...] += theirs

    def finish(chip):
        rows = pl.ds(pl.multiple_of(lax.rem(chip + RING, RING) * 128, 128), 128)
        for h in range(HEADS):
            cols = slice(h * DK, (h + 1) * DK)
            state = entering[cols, :].astype(BF16)
            read = reads[rows, cols] + jnp.dot(q[rows, cols], state, preferred_element_type=F32)
            scale = lax.rsqrt(jnp.mean(read * read, axis=1, keepdims=True) + 1e-6)
            normed[rows, cols] = (read * scale).astype(BF16)

    def give(chip, c, node, side, number, sem):
        go(
            rcopy(
                block(normed, mem(chip, c)),
                ret.at[side, pl.ds(pl.multiple_of(number * CAP, CAP), CAP), :],
                ret_send.at[sem],
                ret_recv.at[side, number],
                {"mem": node},
            )
        )

    finish(z + 4)
    for c in (0, 1):
        give(z + 4, c, mem(z + 5 - 2 * core, c), core, 6, c)
    sem = 2
    for distance in (3, 2):
        for side in (0, 1):
            step = 1 - 2 * side
            finish(z - distance * step)
            for c in (0, 1):
                node = mem(z - (distance - 1) * step, c)
                give(z - distance * step, c, node, side, 2 * (distance - 1) + core, sem)
                sem += 1
    for side in (0, 1):
        chip = z - 1 + 2 * side
        finish(chip)
        give(chip, 1 - core, other, side, 1, sem)
        sem += 1
        ret[side, 0:CAP, :] = block(normed, mem(chip, core))[...]
    finish(z)
    back = go(
        rcopy(
            block(normed, other), own_ret.at[pl.ds(CAP, CAP), :], own_ret_sems.at[0], own_ret_sems.at[1], {"mem": other}
        )
    )
    own_ret[0:CAP, :] = block(normed, me)[...]

    parts = []
    for side in (0, 1):
        for number in range(1, 7):
            rcopy(
                ret.at[side, pl.ds(number * CAP, CAP), :],
                ret.at[side, pl.ds(number * CAP, CAP), :],
                ret_send.at[0],
                ret_recv.at[side, number],
                {"mem": other},
            ).wait_recv()

        def mix(cols, side=side):
            rows = ret[side, :, cols]
            result = jnp.dot(gates[side, 0], rows, preferred_element_type=F32)
            result = result + jnp.dot(gates[side, 1], rows, preferred_element_type=F32)
            part_out[side, :, cols] = result.astype(BF16)

        tiles(HD, 256, mix)
        to = {"mem": mem(z - 1 + 2 * side, core)}
        parts.append(
            go(rcopy(part_out.at[side], part_in.at[side], part_sems.at[0, side], part_sems.at[1, side], to))
        )
    back.wait_recv()
    for part in parts:
        part.wait_recv()

    def last(cols):
        rows = own_ret[:, cols]
        result = jnp.dot(own_gates[0], rows, preferred_element_type=F32)
        result = result + jnp.dot(own_gates[1], rows, preferred_element_type=F32)
        result = result + part_in[0, :, cols].astype(F32) + part_in[1, :, cols].astype(F32)
        out[:, cols] = result.astype(BF16)

    tiles(HD, 256, last)
    for copy in sent:
        copy.wait_send()


def on_device(hidden, routes, gate_levels, query_weight, key_weight, value_weight):
    dma = pltpu.SemaphoreType.DMA
    whole = pl.BlockSpec(memory_space=pl.ANY)
    near = pl.BlockSpec(memory_space=pltpu.VMEM)
    return pl.pallas_call(
        kernel,
        out_shape=jax.ShapeDtypeStruct((TOK, HD), BF16),
        in_specs=[whole, near, near, whole, whole, whole],
        out_specs=near,
        scratch_shapes=[
            pltpu.VMEM((3, TOK, D), BF16),
            pltpu.VMEM((3, 2 * MEMS, TOK), F32),
            pltpu.VMEM((ROWS, D), BF16),
            pltpu.VMEM((2, 7 * CAP, D), BF16),
            pltpu.VMEM((2 * CAP, D), BF16),
            pltpu.VMEM((16, 128, HD), BF16),
            pltpu.VMEM((16, 128, HD), BF16),
            pltpu.VMEM((16, 128, HD), BF16),
            pltpu.VMEM((ROWS, HD), BF16),
            pltpu.VMEM((ROWS, HD), BF16),
            pltpu.VMEM((ROWS, HD), BF16),
            pltpu.VMEM((6 * CAP, D), BF16),
            pltpu.VMEM((HD, DK), F32),
            pltpu.VMEM((HD, DK), F32),
            pltpu.VMEM((3, HD, DK), BF16),
            pltpu.VMEM((4, HD, DK), BF16),
            pltpu.VMEM((4, HD, DK), BF16),
            pltpu.VMEM((ROWS, HD), F32),
            pltpu.VMEM((ROWS, HD), BF16),
            pltpu.VMEM((2, 8 * CAP, HD), BF16),
            pltpu.VMEM((2 * CAP, HD), BF16),
            pltpu.VMEM((2, 2, TOK, 8 * CAP), BF16),
            pltpu.VMEM((2, TOK, 2 * CAP), BF16),
            pltpu.VMEM((2, TOK, HD), BF16),
            pltpu.VMEM((2, TOK, HD), BF16),
            dma((3, 20)),
            dma((3, 20)),
            dma((2, 2)),
            dma((2, 2)),
            dma((2, 7)),
            dma((MEMS,)),
            dma,
            dma((4,)),
            dma((2,)),
            dma((2, 4)),
            dma((12,)),
            dma((2, 7)),
            dma((2,)),
            dma((2, 2)),
        ],
        compiler_params=pltpu.CompilerParams(
            collective_id=0, has_side_effects=True, vmem_limit_bytes=58 * 2**20
        ),
        name="memories",
    )(hidden, routes.T, gate_levels.T, query_weight, key_weight, value_weight)


def solution(mesh):
    return jax.shard_map(
        on_device,
        mesh=mesh,
        in_specs=(
            P(("seq", "mem"), None),
            P(("seq", "mem"), None),
            P(("seq", "mem"), None),
            P("seq", None),
            P("mem", "seq", None),
            P("mem", "seq", None),
        ),
        out_specs=P(("seq", "mem"), None),
        check_vma=False,
    )
```

```python
import jax
import jax.numpy as jnp
from jax import lax
from jax.experimental import pallas as pl
from jax.experimental.pallas import tpu as pltpu
from jax.sharding import PartitionSpec as P

D = 2048
HD = 1024
HEADS = 8
DK = 128
TOK = 256
CAP = 64
MEMS = 16
SIDE = 4
RING = 8
ROWS = MEMS * CAP
HALF = HD // 2
BLOCK = 256
BF16 = jnp.bfloat16
F32 = jnp.float32
MESH = pl.DeviceIdType.MESH


def tiles(total, width, body):
    @pl.loop(0, total // width)
    def _(step):
        body(pl.ds(pl.multiple_of(step * width, width), width))


def weight_stream(whole, own, base, n, x_first, y, x, send_sems, recv_sems):
    f = x_first * x + (1 - x_first) * y
    g = x_first * y + (1 - x_first) * x

    def place(i, j):
        a, b = lax.rem(f + i + SIDE, SIDE), lax.rem(g + j + SIDE, SIDE)
        return x_first * (b * SIDE + a) + (1 - x_first) * (a * SIDE + b)

    def piece(i, j, part=None):
        start, rows = base, n
        if part is not None:
            start, rows = base + part * (n // 2), n // 2
        return whole.at[place(i, j), pl.ds(start, rows), :]

    def send(number, src, dst, i, j):
        return pltpu.make_async_remote_copy(
            src_ref=src,
            dst_ref=dst,
            send_sem=send_sems.at[number],
            recv_sem=recv_sems.at[number],
            device_id={"seq": place(i, j)},
            device_id_type=MESH,
        )

    def relay(number, i, j, part, di, dj):
        return send(number, piece(i, j, part), piece(i, j, part), di, dj)

    first = [send(c, own, piece(0, 0), *to) for c, to in enumerate(((1, 0), (-1, 0), (0, 1), (0, -1)))]
    copies = first + [
        relay(4, -1, 0, 0, 1, 0),
        relay(5, 1, 0, 1, -1, 0),
        relay(6, 0, -1, 0, 0, 1),
        relay(7, 0, 1, 1, 0, -1),
        relay(8, -1, 0, None, 0, 1),
        relay(9, -1, 0, None, 0, -1),
        relay(10, 1, 0, None, 0, 1),
        relay(11, 1, 0, None, 0, -1),
        relay(12, 2, 0, None, 0, 1),
        relay(13, 2, 0, None, 0, -1),
        relay(14, -1, -1, 0, 0, 1),
        relay(15, -1, 1, 1, 0, -1),
        relay(16, 1, -1, 0, 0, 1),
        relay(17, 1, 1, 1, 0, -1),
        relay(18, 2, -1, 0, 0, 1),
        relay(19, 2, 1, 1, 0, -1),
    ]
    return copies


def kernel(
    hid, routes, levels, qw, kw, vw, out,
    raw, tab, rows_in, stage, sib_stage, wq, wk, wv, q, k, v, xs,
    total, entering, part_states, s_send, s_recv, reads, normed,
    ret, own_ret, gates, own_gates, part_out, part_in,
    w_send, w_recv, raw_sems, tab_sems, set_send, set_recv, sib_send, local_sems, swap_sems,
    state_sems, ret_send, ret_recv, own_ret_sems, part_sems,
):
    me, group = lax.axis_index("mem"), lax.axis_index("seq")
    z, core = me // 2, me % 2
    y, x = group // SIDE, group % SIDE

    def mem(chip, c):
        return lax.rem(chip + RING, RING) * 2 + c

    def rcopy(src, dst, send_sem, recv_sem, device):
        return pltpu.make_async_remote_copy(
            src_ref=src, dst_ref=dst, send_sem=send_sem, recv_sem=recv_sem, device_id=device, device_id_type=MESH
        )

    def spot(source):
        return pl.ds(pl.multiple_of(source * CAP, CAP), CAP)

    def columns(part):
        return pl.ds(part * HD, HD)

    sent = []

    def go(copy):
        copy.start()
        sent.append(copy)
        return copy

    other = mem(z, 1 - core)
    barrier = pltpu.get_barrier_semaphore()
    peers = [{"mem": other}]
    peers += [{"mem": mem(z + d, c)} for d in (-3, -2, -1, 1, 2, 3) for c in (0, 1)]
    for dx, dy in ((1, 0), (3, 0), (0, 1), (0, 3)):
        peers.append({"seq": lax.rem(y + dy, SIDE) * SIDE + lax.rem(x + dx, SIDE)})
    for peer in peers:
        pl.semaphore_signal(barrier, inc=1, device_id=peer, device_id_type=MESH)

    mine = [
        pltpu.make_async_copy(hid, raw.at[2], local_sems.at[0]),
        pltpu.make_async_copy(kw.at[0], wk.at[group], local_sems.at[1]),
        pltpu.make_async_copy(vw.at[0], wv.at[group], local_sems.at[2]),
    ]
    half = pl.multiple_of(core * CAP, CAP)
    mine.append(
        pltpu.make_async_copy(qw.at[pl.ds(half, CAP), :], wq.at[group, pl.ds(half, CAP), :], local_sems.at[3])
    )
    for copy in mine:
        copy.start()
    ids = lax.broadcasted_iota(jnp.int32, (MEMS, TOK), 0)
    hit0, hit1 = routes[0:1, :] == ids, routes[1:2, :] == ids
    earlier = lax.broadcasted_iota(jnp.int32, (TOK, TOK), 0) < lax.broadcasted_iota(jnp.int32, (TOK, TOK), 1)
    hits = jnp.where(hit0 | hit1, 1.0, 0.0)
    place = jnp.dot(hits.astype(BF16), jnp.where(earlier, 1.0, 0.0).astype(BF16), preferred_element_type=F32)
    lev0, lev1 = levels[0:1, :].astype(F32), levels[1:2, :].astype(F32)
    both = lev0 + lev1
    tab[2, 0:MEMS, :] = jnp.where(hits > 0, place, -1.0)
    tab[2, MEMS : 2 * MEMS, :] = jnp.where(hit0, lev0 / both, 0.0) + jnp.where(hit1, lev1 / both, 0.0)

    pl.semaphore_wait(barrier, len(peers))

    raws, tabs = [], []
    for side, step in ((0, 1), (1, -1)):
        to = {"mem": mem(z + step, core)}
        tabs.append(go(rcopy(tab.at[2], tab.at[side], tab_sems.at[0, side], tab_sems.at[1, side], to)))
    for part in (0, 1):
        for side, step in ((0, 1), (1, -1)):
            cols, sems = columns(part), raw_sems.at[side, part]
            to = {"mem": mem(z + step, core)}
            raws.append(go(rcopy(hid.at[:, cols], raw.at[side, :, cols], sems.at[0], sems.at[1], to)))
    own_q = qw.at[pl.ds(half, CAP), :]
    keyed = [
        weight_stream(wk, kw.at[0], 0, 128, 1, y, x, w_send.at[0], w_recv.at[0]),
        weight_stream(wv, vw.at[0], 0, 128, 0, y, x, w_send.at[1], w_recv.at[1]),
    ]
    asked = [weight_stream(wq, own_q, half, CAP, 1 - core, y, x, w_send.at[2], w_recv.at[2])]

    def start(streams, *numbers):
        for number in numbers:
            for copies in streams:
                go(copies[number])

    def arrive(streams, *numbers):
        for number in numbers:
            for copies in streams:
                copies[number].wait_recv()

    start(keyed, 0, 1, 2, 3)

    slot = lax.broadcasted_iota(jnp.int32, (CAP, TOK), 0).astype(F32)

    def matches(index, mems):
        return [slot == tab[index, pl.ds(e, 1), :] for e in mems]

    def chosen(index, mems):
        ones = [jnp.where(m, 1.0, 0.0).astype(BF16) for m in matches(index, mems)]
        return jnp.concatenate(ones, axis=0)

    def pack(index, ones, dest, part):
        def body(cols):
            cols = pl.ds(part * HD + cols.start, cols.size)
            dest[:, cols] = jnp.dot(ones, raw[index, :, cols], preferred_element_type=F32).astype(BF16)

        tiles(HD, 512, body)

    def mixing(index, mems, dest, width):
        parts = [
            jnp.where(m, tab[index, pl.ds(MEMS + e, 1), :], 0.0) for m, e in zip(matches(index, mems), mems)
        ]
        if width > len(mems) * CAP:
            parts.append(jnp.zeros((width - len(mems) * CAP, TOK), F32))
        weights = jnp.concatenate(parts, axis=0).T
        high = weights.astype(BF16)
        dest[0] = high
        dest[1] = (weights - high.astype(F32)).astype(BF16)

    def served(side):
        step = 1 - 2 * side
        return [
            me, other,
            mem(z + step, 0), mem(z + step, 1),
            mem(z + 2 * step, 0), mem(z + 2 * step, 1),
            mem(z + 3 * step, side),
        ]

    for copy in mine:
        copy.wait()
    for part in (0, 1):
        pack(2, chosen(2, [me, other]), sib_stage, part)
    for part in (0, 1):
        cols = columns(part)
        src, dst = sib_stage.at[pl.ds(CAP, CAP), cols], rows_in.at[spot(me), cols]
        go(rcopy(src, dst, sib_send.at[part], set_recv.at[me, part], {"mem": other}))
    rows_in[spot(me), :] = sib_stage[0:CAP, :]
    mixing(2, [me, other], own_gates, 2 * CAP)

    arrive(keyed, 0, 1, 2, 3)
    start(keyed, 8, 9, 10, 11, 4, 5, 6, 7)
    start(asked, 0, 1, 2, 3)

    for side in (0, 1):
        tabs[side].wait_recv()
    for part in (0, 1):
        for side in (0, 1):
            origin = mem(z - 1 + 2 * side, core)
            mems = served(side)
            cols = columns(part)
            raws[2 * part + side].wait_recv()
            pack(side, chosen(side, mems), stage.at[side], part)
            for number in (2, 3, 4, 5, 6, 1):
                src, dst = stage.at[side, pl.ds(number * CAP, CAP), cols], rows_in.at[spot(origin), cols]
                sems = (set_send.at[side, number, part], set_recv.at[origin, part])
                go(rcopy(src, dst, *sems, {"mem": mems[number]}))
            rows_in[spot(origin), cols] = stage[side, 0:CAP, cols]

    arrive(keyed, 4, 5, 8, 9, 10, 11)
    start(keyed, 12, 13, 14, 15, 16, 17)
    arrive(asked, 0, 1, 2, 3)
    start(asked, 8, 9, 10, 11, 4, 5, 6, 7)
    for side in (0, 1):
        mixing(side, served(side), gates.at[side], 8 * CAP)
        ret[side, :, 7 * CAP : 8 * CAP, :] = jnp.zeros((2, CAP, HALF), BF16)
    arrive(keyed, 12, 13)
    start(keyed, 18, 19)
    arrive(asked, 4, 5, 8, 9, 10, 11)
    start(asked, 12, 13, 14, 15, 16, 17)
    arrive(keyed, 6, 7, 14, 15, 16, 17, 18, 19)

    def take(first, sources, wait):
        for n, source in enumerate(sources):
            if wait[n]:
                for part in (0, 1):
                    there = rows_in.at[spot(source), columns(part)]
                    rcopy(there, there, sib_send.at[part], set_recv.at[source, part], {"mem": other}).wait_recv()
            xs[first + n * CAP : first + (n + 1) * CAP, :] = rows_in[spot(source), :]

    def project(first, sources, weight, dest):
        many = len(sources) * CAP
        width = HD if many <= 384 else HALF

        def body(cols):
            w = weight[:, :, cols].reshape(D, width)
            result = jnp.dot(xs[first : first + many, :], w, preferred_element_type=F32).astype(BF16)
            for n, source in enumerate(sources):
                dest[spot(source), cols] = result[n * CAP : (n + 1) * CAP]

        tiles(HD, width, body)

    near = [me, other] + [mem(z + d, c) for d in (-1, 1) for c in (core, 1 - core)]
    take(0, near, [False, True, False, True, False, True])
    project(0, near, wk, k)
    arrive(asked, 12, 13)
    start(asked, 18, 19)
    project(0, near, wv, v)
    arrive(asked, 6, 7, 14, 15, 16, 17, 18, 19)
    halves = wq.at[:, pl.ds(half, CAP), :]
    swap = go(rcopy(halves, halves, swap_sems.at[0], swap_sems.at[1], {"mem": other}))
    middle = [mem(z + d, c) for d in (-2, 2) for c in (0, 1)]
    take(384, middle, [True] * 4)
    project(384, middle, wk, k)
    project(384, middle, wv, v)
    swap.wait_recv()
    project(0, near + middle, wq, q)
    far = [mem(z + d, c) for d in (-3, 3) for c in (0, 1)]
    take(640, far, [True] * 4)
    project(640, far, wk, k)
    project(640, far, wv, v)
    last_ones = [mem(z + 4, c) for c in (0, 1)]
    take(896, last_ones, [True] * 2)
    project(896, last_ones, wk, k)
    project(896, last_ones, wv, v)

    @pl.loop(0, HEADS)
    def _(h):
        cols = pl.ds(pl.multiple_of(h * DK, DK), DK)
        running = jnp.zeros((DK, DK), F32)
        for b in range(ROWS // BLOCK):
            if b:
                part_states[b - 1, cols, :] = running.astype(BF16)
            rows = slice(b * BLOCK, (b + 1) * BLOCK)
            running = running + lax.dot_general(
                k[rows, cols], v[rows, cols], (((0,), (0,)), ((), ())), preferred_element_type=F32
            )
        total[cols, :] = running

    causal = lax.broadcasted_iota(jnp.int32, (BLOCK, BLOCK), 0) >= lax.broadcasted_iota(
        jnp.int32, (BLOCK, BLOCK), 1
    )

    def attend(low, high):
        @pl.loop(low, high)
        def _(h):
            cols = pl.ds(pl.multiple_of(h * DK, DK), DK)
            for b in range(ROWS // BLOCK):
                rows = slice(b * BLOCK, (b + 1) * BLOCK)
                queries = q[rows, cols]
                scores = lax.dot_general(
                    queries, k[rows, cols], (((1,), (1,)), ((), ())), preferred_element_type=F32
                )
                scores = jnp.where(causal, scores, 0.0).astype(BF16)
                read = jnp.dot(scores, v[rows, cols], preferred_element_type=F32)
                if b:
                    read = read + jnp.dot(queries, part_states[b - 1, cols, :], preferred_element_type=F32)
                reads[rows, cols] = read

    def at(row, column):
        return row * SIDE + column

    y1, y3 = y + 1 - 2 * (y % 2), SIDE - 1 - y
    x1, x3 = x + 1 - 2 * (x % 2), SIDE - 1 - x
    sums = [(at(y, x1), x % 2), (at(y, x3), x // 2), (at(y1, x), y % 2), (at(y3, x), y // 2)]
    befores = [(at(y3, x), 1 - y // 2), (at(y1, x), 1 - y % 2), (at(y, x3), 1 - x // 2), (at(y, x1), 1 - x % 2)]
    low, high = slice(0, HALF), slice(HALF, HD)
    entering[...] = jnp.zeros_like(entering)
    for step in range(4):
        s_send[step, low] = total[low].astype(BF16)
        s_send[step, high] = (entering[high] + total[high] * befores[step][1].astype(F32)).astype(BF16)
        copies = []
        for stream, (rows, to) in enumerate(((low, sums[step][0]), (high, befores[step][0]))):
            there = pl.ds(rows.start, HALF)
            sems = state_sems.at[step, stream]
            src, dst = s_send.at[step, there], s_recv.at[step, there]
            copies.append(go(rcopy(src, dst, sems.at[0], sems.at[1], {"seq": to})))
        if step == 0:
            project(640, far + last_ones, wq, q)
        attend(2 * step, 2 * step + 2)
        for copy in copies:
            copy.wait_recv()
        theirs = s_recv[step, low].astype(F32)
        entering[low] += theirs * sums[step][1].astype(F32)
        if step < 3:
            total[low] += theirs
        entering[high] += s_recv[step, high].astype(F32)

    def finish(chip, part):
        rows = pl.ds(pl.multiple_of(lax.rem(chip + RING, RING) * 128, 128), 128)
        for h in range(part * HEADS // 2, (part + 1) * HEADS // 2):
            cols = slice(h * DK, (h + 1) * DK)
            state = entering[cols, :].astype(BF16)
            read = reads[rows, cols] + jnp.dot(q[rows, cols], state, preferred_element_type=F32)
            scale = lax.rsqrt(jnp.mean(read * read, axis=1, keepdims=True) + 1e-6)
            normed[part, rows, cols.start - part * HALF : cols.stop - part * HALF] = (read * scale).astype(BF16)

    def give(part, source, node, side, number, sem):
        src, dst = normed.at[part, spot(source)], ret.at[side, part, spot(number)]
        go(rcopy(src, dst, ret_send.at[sem, part], ret_recv.at[side, number, part], {"mem": node}))

    back = []
    for part in (0, 1):
        finish(z + 4, part)
        for c in (0, 1):
            give(part, mem(z + 4, c), mem(z + 5 - 2 * core, c), core, 6, c)
        sem = 2
        for distance in (3, 2):
            for side in (0, 1):
                step = 1 - 2 * side
                finish(z - distance * step, part)
                for c in (0, 1):
                    source, node = mem(z - distance * step, c), mem(z - (distance - 1) * step, c)
                    give(part, source, node, side, 2 * (distance - 1) + core, sem)
                    sem += 1
        for side in (0, 1):
            chip = z - 1 + 2 * side
            finish(chip, part)
            give(part, mem(chip, 1 - core), other, side, 1, sem)
            sem += 1
            ret[side, part, 0:CAP, :] = normed[part, spot(mem(chip, core)), :]
        finish(z, part)
        src, dst = normed.at[part, spot(other)], own_ret.at[part, pl.ds(CAP, CAP), :]
        back.append(go(rcopy(src, dst, own_ret_sems.at[part, 0], own_ret_sems.at[part, 1], {"mem": other})))
        own_ret[part, 0:CAP, :] = normed[part, spot(me), :]

    parts = []
    for part in (0, 1):
        for side in (0, 1):
            for number in range(1, 7):
                there = ret.at[side, part, pl.ds(number * CAP, CAP), :]
                sems = (ret_send.at[0, 0], ret_recv.at[side, number, part])
                rcopy(there, there, *sems, {"mem": other}).wait_recv()
            rows = ret[side, part]
            result = jnp.dot(gates[side, 0], rows, preferred_element_type=F32)
            result = result + jnp.dot(gates[side, 1], rows, preferred_element_type=F32)
            part_out[side, part] = result.astype(BF16)
            to = {"mem": mem(z - 1 + 2 * side, core)}
            src, dst, sems = part_out.at[side, part], part_in.at[side, part], part_sems.at[side, part]
            parts.append(go(rcopy(src, dst, sems.at[0], sems.at[1], to)))
    for part in (0, 1):
        back[part].wait_recv()
        rows = own_ret[part]
        result = jnp.dot(own_gates[0], rows, preferred_element_type=F32)
        result = result + jnp.dot(own_gates[1], rows, preferred_element_type=F32)
        for side in (0, 1):
            parts[2 * part + side].wait_recv()
        result = result + part_in[0, part].astype(F32) + part_in[1, part].astype(F32)
        out[:, part * HALF : (part + 1) * HALF] = result.astype(BF16)
    for copy in sent:
        copy.wait_send()


def on_device(hidden, routes, gate_levels, query_weight, key_weight, value_weight):
    dma = pltpu.SemaphoreType.DMA
    whole = pl.BlockSpec(memory_space=pl.ANY)
    near = pl.BlockSpec(memory_space=pltpu.VMEM)
    return pl.pallas_call(
        kernel,
        out_shape=jax.ShapeDtypeStruct((TOK, HD), BF16),
        in_specs=[whole, near, near, whole, whole, whole],
        out_specs=near,
        scratch_shapes=[
            pltpu.VMEM((3, TOK, D), BF16),
            pltpu.VMEM((3, 2 * MEMS, TOK), F32),
            pltpu.VMEM((ROWS, D), BF16),
            pltpu.VMEM((2, 7 * CAP, D), BF16),
            pltpu.VMEM((2 * CAP, D), BF16),
            pltpu.VMEM((16, 128, HD), BF16),
            pltpu.VMEM((16, 128, HD), BF16),
            pltpu.VMEM((16, 128, HD), BF16),
            pltpu.VMEM((ROWS, HD), BF16),
            pltpu.VMEM((ROWS, HD), BF16),
            pltpu.VMEM((ROWS, HD), BF16),
            pltpu.VMEM((ROWS, D), BF16),
            pltpu.VMEM((HD, DK), F32),
            pltpu.VMEM((HD, DK), F32),
            pltpu.VMEM((3, HD, DK), BF16),
            pltpu.VMEM((4, HD, DK), BF16),
            pltpu.VMEM((4, HD, DK), BF16),
            pltpu.VMEM((ROWS, HD), F32),
            pltpu.VMEM((2, ROWS, HALF), BF16),
            pltpu.VMEM((2, 2, 8 * CAP, HALF), BF16),
            pltpu.VMEM((2, 2 * CAP, HALF), BF16),
            pltpu.VMEM((2, 2, TOK, 8 * CAP), BF16),
            pltpu.VMEM((2, TOK, 2 * CAP), BF16),
            pltpu.VMEM((2, 2, TOK, HALF), BF16),
            pltpu.VMEM((2, 2, TOK, HALF), BF16),
            dma((3, 20)),
            dma((3, 20)),
            dma((2, 2, 2)),
            dma((2, 2)),
            dma((2, 7, 2)),
            dma((MEMS, 2)),
            dma((2,)),
            dma((4,)),
            dma((2,)),
            dma((4, 2, 2)),
            dma((12, 2)),
            dma((2, 7, 2)),
            dma((2, 2)),
            dma((2, 2, 2)),
        ],
        compiler_params=pltpu.CompilerParams(
            collective_id=0, has_side_effects=True, vmem_limit_bytes=58 * 2**20
        ),
        name="memories",
    )(hidden, routes.T, gate_levels.T, query_weight, key_weight, value_weight)


def solution(mesh):
    return jax.shard_map(
        on_device,
        mesh=mesh,
        in_specs=(
            P(("seq", "mem"), None),
            P(("seq", "mem"), None),
            P(("seq", "mem"), None),
            P("seq", None),
            P("mem", "seq", None),
            P("mem", "seq", None),
        ),
        out_specs=P(("seq", "mem"), None),
        check_vma=False,
    )
```

```python
import jax
import jax.numpy as jnp
from jax import lax
from jax.experimental import pallas as pl
from jax.experimental.pallas import tpu as pltpu
from jax.sharding import PartitionSpec as P

D = 2048
HD = 1024
HEADS = 8
DK = 128
TOK = 256
CAP = 64
MEMS = 16
SIDE = 4
RING = 8
ROWS = MEMS * CAP
HALF = HD // 2
PARTS = 4
PART = HD // PARTS
BLOCK = 256
BF16 = jnp.bfloat16
F32 = jnp.float32
MESH = pl.DeviceIdType.MESH


def tiles(total, width, body):
    @pl.loop(0, total // width)
    def _(step):
        body(pl.ds(pl.multiple_of(step * width, width), width))


def weight_stream(whole, own, base, n, x_first, y, x, send_sems, recv_sems):
    f = x_first * x + (1 - x_first) * y
    g = x_first * y + (1 - x_first) * x

    def place(i, j):
        a, b = lax.rem(f + i + SIDE, SIDE), lax.rem(g + j + SIDE, SIDE)
        return x_first * (b * SIDE + a) + (1 - x_first) * (a * SIDE + b)

    def piece(i, j, part=None):
        start, rows = base, n
        if part is not None:
            start, rows = base + part * (n // 2), n // 2
        return whole.at[place(i, j), pl.ds(start, rows), :]

    def send(number, src, dst, i, j):
        return pltpu.make_async_remote_copy(
            src_ref=src,
            dst_ref=dst,
            send_sem=send_sems.at[number],
            recv_sem=recv_sems.at[number],
            device_id={"seq": place(i, j)},
            device_id_type=MESH,
        )

    def relay(number, i, j, part, di, dj):
        return send(number, piece(i, j, part), piece(i, j, part), di, dj)

    first = [send(c, own, piece(0, 0), *to) for c, to in enumerate(((1, 0), (-1, 0), (0, 1), (0, -1)))]
    copies = first + [
        relay(4, -1, 0, 0, 1, 0),
        relay(5, 1, 0, 1, -1, 0),
        relay(6, 0, -1, 0, 0, 1),
        relay(7, 0, 1, 1, 0, -1),
        relay(8, -1, 0, None, 0, 1),
        relay(9, -1, 0, None, 0, -1),
        relay(10, 1, 0, None, 0, 1),
        relay(11, 1, 0, None, 0, -1),
        relay(12, 2, 0, None, 0, 1),
        relay(13, 2, 0, None, 0, -1),
        relay(14, -1, -1, 0, 0, 1),
        relay(15, -1, 1, 1, 0, -1),
        relay(16, 1, -1, 0, 0, 1),
        relay(17, 1, 1, 1, 0, -1),
        relay(18, 2, -1, 0, 0, 1),
        relay(19, 2, 1, 1, 0, -1),
    ]
    return copies


def kernel(
    hid, routes, levels, qw, kw, vw, out,
    raw, tab, rows_in, stage, sib_stage, wq, wk, wv, q, k, v, xs,
    block_states, total, entering, before, s_send, s_recv, reads, normed,
    ret, own_ret, gates, own_gates, part_out, part_in,
    w_send, w_recv, raw_sems, tab_sems, set_send, set_recv, sib_send, local_sems, swap_sems,
    state_sems, ret_send, ret_recv, own_ret_sems, part_sems,
):
    me, group = lax.axis_index("mem"), lax.axis_index("seq")
    z, core = me // 2, me % 2
    y, x = group // SIDE, group % SIDE

    def mem(chip, c):
        return lax.rem(chip + RING, RING) * 2 + c

    def rcopy(src, dst, send_sem, recv_sem, device):
        return pltpu.make_async_remote_copy(
            src_ref=src, dst_ref=dst, send_sem=send_sem, recv_sem=recv_sem, device_id=device, device_id_type=MESH
        )

    def spot(source):
        return pl.ds(pl.multiple_of(source * CAP, CAP), CAP)

    def columns(part):
        return pl.ds(part * HD, HD)

    sent = []

    def go(copy):
        copy.start()
        sent.append(copy)
        return copy

    other = mem(z, 1 - core)
    barrier = pltpu.get_barrier_semaphore()
    peers = [{"mem": other}]
    peers += [{"mem": mem(z + d, c)} for d in (-3, -2, -1, 1, 2, 3) for c in (0, 1)]
    for dx, dy in ((1, 0), (3, 0), (0, 1), (0, 3)):
        peers.append({"seq": lax.rem(y + dy, SIDE) * SIDE + lax.rem(x + dx, SIDE)})
    for peer in peers:
        pl.semaphore_signal(barrier, inc=1, device_id=peer, device_id_type=MESH)

    mine = [
        pltpu.make_async_copy(hid, raw.at[2], local_sems.at[0]),
        pltpu.make_async_copy(kw.at[0], wk.at[group], local_sems.at[1]),
        pltpu.make_async_copy(vw.at[0], wv.at[group], local_sems.at[2]),
    ]
    half = pl.multiple_of(core * CAP, CAP)
    mine.append(
        pltpu.make_async_copy(qw.at[pl.ds(half, CAP), :], wq.at[group, pl.ds(half, CAP), :], local_sems.at[3])
    )
    for copy in mine:
        copy.start()
    ids = lax.broadcasted_iota(jnp.int32, (MEMS, TOK), 0)
    hit0, hit1 = routes[0:1, :] == ids, routes[1:2, :] == ids
    earlier = lax.broadcasted_iota(jnp.int32, (TOK, TOK), 0) < lax.broadcasted_iota(jnp.int32, (TOK, TOK), 1)
    hits = jnp.where(hit0 | hit1, 1.0, 0.0)
    place = jnp.dot(hits.astype(BF16), jnp.where(earlier, 1.0, 0.0).astype(BF16), preferred_element_type=F32)
    lev0, lev1 = levels[0:1, :].astype(F32), levels[1:2, :].astype(F32)
    both = lev0 + lev1
    tab[2, 0:MEMS, :] = jnp.where(hits > 0, place, -1.0)
    tab[2, MEMS : 2 * MEMS, :] = jnp.where(hit0, lev0 / both, 0.0) + jnp.where(hit1, lev1 / both, 0.0)

    pl.semaphore_wait(barrier, len(peers))

    raws, tabs = [], []
    for side, step in ((0, 1), (1, -1)):
        to = {"mem": mem(z + step, core)}
        tabs.append(go(rcopy(tab.at[2], tab.at[side], tab_sems.at[0, side], tab_sems.at[1, side], to)))
    for part in (0, 1):
        for side, step in ((0, 1), (1, -1)):
            cols, sems = columns(part), raw_sems.at[side, part]
            to = {"mem": mem(z + step, core)}
            raws.append(go(rcopy(hid.at[:, cols], raw.at[side, :, cols], sems.at[0], sems.at[1], to)))
    own_q = qw.at[pl.ds(half, CAP), :]
    keyed = [
        weight_stream(wk, kw.at[0], 0, 128, 1, y, x, w_send.at[0], w_recv.at[0]),
        weight_stream(wv, vw.at[0], 0, 128, 0, y, x, w_send.at[1], w_recv.at[1]),
    ]
    asked = [weight_stream(wq, own_q, half, CAP, 1 - core, y, x, w_send.at[2], w_recv.at[2])]

    def start(streams, *numbers):
        for number in numbers:
            for copies in streams:
                go(copies[number])

    def arrive(streams, *numbers):
        for number in numbers:
            for copies in streams:
                copies[number].wait_recv()

    start(keyed, 0, 1, 2, 3)

    slot = lax.broadcasted_iota(jnp.int32, (CAP, TOK), 0).astype(F32)

    def matches(index, mems):
        return [slot == tab[index, pl.ds(e, 1), :] for e in mems]

    def chosen(index, mems):
        ones = [jnp.where(m, 1.0, 0.0).astype(BF16) for m in matches(index, mems)]
        return jnp.concatenate(ones, axis=0)

    def pack(index, ones, dest, part):
        def body(cols):
            cols = pl.ds(part * HD + cols.start, cols.size)
            dest[:, cols] = jnp.dot(ones, raw[index, :, cols], preferred_element_type=F32).astype(BF16)

        tiles(HD, 512, body)

    def mixing(index, mems, dest, width):
        parts = [
            jnp.where(m, tab[index, pl.ds(MEMS + e, 1), :], 0.0) for m, e in zip(matches(index, mems), mems)
        ]
        if width > len(mems) * CAP:
            parts.append(jnp.zeros((width - len(mems) * CAP, TOK), F32))
        weights = jnp.concatenate(parts, axis=0).T
        high = weights.astype(BF16)
        dest[0] = high
        dest[1] = (weights - high.astype(F32)).astype(BF16)

    def served(side):
        step = 1 - 2 * side
        return [
            me, other,
            mem(z + step, 0), mem(z + step, 1),
            mem(z + 2 * step, 0), mem(z + 2 * step, 1),
            mem(z + 3 * step, side),
        ]

    for copy in mine:
        copy.wait()
    for part in (0, 1):
        pack(2, chosen(2, [me, other]), sib_stage, part)
    for part in (0, 1):
        cols = columns(part)
        src, dst = sib_stage.at[pl.ds(CAP, CAP), cols], rows_in.at[spot(me), cols]
        go(rcopy(src, dst, sib_send.at[part], set_recv.at[me, part], {"mem": other}))
    rows_in[spot(me), :] = sib_stage[0:CAP, :]
    mixing(2, [me, other], own_gates, 2 * CAP)

    arrive(keyed, 0, 1, 2, 3)
    start(keyed, 8, 9, 10, 11, 4, 5, 6, 7)
    start(asked, 0, 1, 2, 3)

    for side in (0, 1):
        tabs[side].wait_recv()
    for part in (0, 1):
        for side in (0, 1):
            origin = mem(z - 1 + 2 * side, core)
            mems = served(side)
            cols = columns(part)
            raws[2 * part + side].wait_recv()
            pack(side, chosen(side, mems), stage.at[side], part)
            for number in (2, 3, 4, 5, 6, 1):
                src, dst = stage.at[side, pl.ds(number * CAP, CAP), cols], rows_in.at[spot(origin), cols]
                sems = (set_send.at[side, number, part], set_recv.at[origin, part])
                go(rcopy(src, dst, *sems, {"mem": mems[number]}))
            rows_in[spot(origin), cols] = stage[side, 0:CAP, cols]

    arrive(keyed, 4, 5, 8, 9, 10, 11)
    start(keyed, 12, 13, 14, 15, 16, 17)
    arrive(asked, 0, 1, 2, 3)
    start(asked, 8, 9, 10, 11, 4, 5, 6, 7)
    for side in (0, 1):
        mixing(side, served(side), gates.at[side], 8 * CAP)
        ret[side, :, 7 * CAP : 8 * CAP, :] = jnp.zeros((PARTS, CAP, PART), BF16)
    arrive(keyed, 12, 13)
    start(keyed, 18, 19)
    arrive(asked, 4, 5, 8, 9, 10, 11)
    start(asked, 12, 13, 14, 15, 16, 17)
    arrive(keyed, 6, 7, 14, 15, 16, 17, 18, 19)

    def take(first, sources, wait):
        for n, source in enumerate(sources):
            if wait[n]:
                for part in (0, 1):
                    there = rows_in.at[spot(source), columns(part)]
                    rcopy(there, there, sib_send.at[part], set_recv.at[source, part], {"mem": other}).wait_recv()
            xs[first + n * CAP : first + (n + 1) * CAP, :] = rows_in[spot(source), :]

    def project(first, sources, weight, dest):
        many = len(sources) * CAP
        width = HD if many <= 384 else HALF

        def body(cols):
            w = weight[:, :, cols].reshape(D, width)
            result = jnp.dot(xs[first : first + many, :], w, preferred_element_type=F32).astype(BF16)
            for n, source in enumerate(sources):
                dest[spot(source), cols] = result[n * CAP : (n + 1) * CAP]

        tiles(HD, width, body)

    causal = lax.broadcasted_iota(jnp.int32, (BLOCK, BLOCK), 0) >= lax.broadcasted_iota(
        jnp.int32, (BLOCK, BLOCK), 1
    )
    first_block = lax.rem((z + 1) // 2 + 3, 4)
    turn = [lax.rem(first_block + n, 4) for n in range(4)]

    def head_cols(h):
        return pl.ds(pl.multiple_of(h * DK, DK), DK)

    def state_rows(h):
        return pl.ds(pl.multiple_of((lax.rem(h, 2) * (HEADS // 2) + h // 2) * DK, DK), DK)

    def attend(blocks, h):
        cols = head_cols(h)
        for b in blocks:
            rows = pl.ds(pl.multiple_of(b * BLOCK, BLOCK), BLOCK)
            scores = lax.dot_general(
                q[rows, cols], k[rows, cols], (((1,), (1,)), ((), ())), preferred_element_type=F32
            )
            scores = jnp.where(causal, scores, 0.0).astype(BF16)
            reads[rows, cols] = jnp.dot(scores, v[rows, cols], preferred_element_type=F32)

    def add_up(blocks, h):
        cols = head_cols(h)
        for b in blocks:
            rows = pl.ds(pl.multiple_of(b * BLOCK, BLOCK), BLOCK)
            block_states[b, state_rows(h), :] = lax.dot_general(
                k[rows, cols], v[rows, cols], (((0,), (0,)), ((), ())), preferred_element_type=F32
            )

    near = [me, other] + [mem(z + d, c) for d in (-1, 1) for c in (core, 1 - core)]
    take(0, near, [False, True, False, True, False, True])
    project(0, near, wk, k)
    arrive(asked, 12, 13)
    start(asked, 18, 19)
    project(0, near, wv, v)
    arrive(asked, 6, 7, 14, 15, 16, 17, 18, 19)
    halves = wq.at[:, pl.ds(half, CAP), :]
    swap = go(rcopy(halves, halves, swap_sems.at[0], swap_sems.at[1], {"mem": other}))
    middle = [mem(z + d, c) for d in (-2, 2) for c in (0, 1)]
    take(384, middle, [True] * 4)
    project(384, middle, wk, k)
    project(384, middle, wv, v)
    swap.wait_recv()
    project(0, near + middle, wq, q)

    @pl.loop(0, HEADS)
    def _(h):
        add_up(turn[:2], h)

    @pl.loop(0, HEADS)
    def _(h):
        attend(turn[:2], h)

    far = [mem(z + d, c) for d in (-3, 3) for c in (0, 1)]
    take(640, far, [True] * 4)
    project(640, far, wk, k)
    project(640, far, wv, v)
    last_ones = [mem(z + 4, c) for c in (0, 1)]
    take(896, last_ones, [True] * 2)
    project(896, last_ones, wk, k)
    project(896, last_ones, wv, v)

    @pl.loop(0, HEADS)
    def _(h):
        add_up(turn[2:], h)
        rows = state_rows(h)
        total[rows, :] = (block_states[0, rows, :] + block_states[1, rows, :]) + (
            block_states[2, rows, :] + block_states[3, rows, :]
        )

    def at(row, column):
        return row * SIDE + column

    y1, y3 = y + 1 - 2 * (y % 2), SIDE - 1 - y
    x1, x3 = x + 1 - 2 * (x % 2), SIDE - 1 - x
    sums = [(at(y, x1), x % 2), (at(y, x3), x // 2), (at(y1, x), y % 2), (at(y3, x), y // 2)]
    befores = [(at(y3, x), 1 - y // 2), (at(y1, x), 1 - y % 2), (at(y, x3), 1 - x // 2), (at(y, x1), 1 - x % 2)]
    entering[...] = jnp.zeros_like(entering)
    moving = {}

    def low_high(pair):
        return pl.ds(pair * PART, PART), pl.ds(HALF + pair * PART, PART)

    def push(step, pair):
        low, high = low_high(pair)
        s_send[step, low, :] = total[low, :].astype(BF16)
        s_send[step, high, :] = (entering[high, :] + total[high, :] * befores[step][1].astype(F32)).astype(BF16)
        for stream, (rows, to) in enumerate(((low, sums[step][0]), (high, befores[step][0]))):
            sems = state_sems.at[step, pair, stream]
            src, dst = s_send.at[step, rows], s_recv.at[step, rows]
            moving[step, pair, stream] = go(rcopy(src, dst, sems.at[0], sems.at[1], {"seq": to}))

    def pull(step, pair):
        low, high = low_high(pair)
        moving[step, pair, 0].wait_recv()
        moving[step, pair, 1].wait_recv()
        theirs = s_recv[step, low, :].astype(F32)
        entering[low, :] += theirs * sums[step][1].astype(F32)
        if step < 3:
            total[low, :] += theirs
        entering[high, :] += s_recv[step, high, :].astype(F32)

    push(0, 0)
    push(0, 1)
    project(640, far + last_ones, wq, q)
    running = jnp.zeros((HD, DK), F32)
    for b in range(4):
        before[b] = running.astype(BF16)
        running = running + block_states[b]
    for step in range(3):
        for pair in (0, 1):
            for h in ((0, 1), (2,), (3, 4), (5,), (6,), (7,))[2 * step + pair]:
                attend(turn[2:], h)
            pull(step, pair)
            push(step + 1, pair)
    pull(3, 0)

    def finish(chip, part):
        chip = lax.rem(chip + RING, RING)
        rows = pl.ds(pl.multiple_of(chip * 128, 128), 128)
        for h in (2 * part, 2 * part + 1):
            cols = slice(h * DK, (h + 1) * DK)
            place = h % 2 * (HEADS // 2) + h // 2
            states = slice(place * DK, (place + 1) * DK)
            state = (entering[states, :] + before[chip // 2, states, :].astype(F32)).astype(BF16)
            read = reads[rows, cols] + jnp.dot(q[rows, cols], state, preferred_element_type=F32)
            scale = lax.rsqrt(jnp.mean(read * read, axis=1, keepdims=True) + 1e-6)
            normed[part, rows, h % 2 * DK : (h % 2 + 1) * DK] = (read * scale).astype(BF16)

    def give(part, source, node, side, number, sem):
        src, dst = normed.at[part, spot(source)], ret.at[side, part, spot(number)]
        go(rcopy(src, dst, ret_send.at[sem, part], ret_recv.at[side, number, part], {"mem": node}))

    back = []
    for part in range(PARTS):
        if part == 2:
            pull(3, 1)
        finish(z + 4, part)
        for c in (0, 1):
            give(part, mem(z + 4, c), mem(z + 5 - 2 * core, c), core, 6, c)
        sem = 2
        for distance in (3, 2):
            for side in (0, 1):
                step = 1 - 2 * side
                finish(z - distance * step, part)
                for c in (0, 1):
                    source, node = mem(z - distance * step, c), mem(z - (distance - 1) * step, c)
                    give(part, source, node, side, 2 * (distance - 1) + core, sem)
                    sem += 1
        for side in (0, 1):
            chip = z - 1 + 2 * side
            finish(chip, part)
            give(part, mem(chip, 1 - core), other, side, 1, sem)
            sem += 1
            ret[side, part, 0:CAP, :] = normed[part, spot(mem(chip, core)), :]
        finish(z, part)
        src, dst = normed.at[part, spot(other)], own_ret.at[part, pl.ds(CAP, CAP), :]
        back.append(go(rcopy(src, dst, own_ret_sems.at[part, 0], own_ret_sems.at[part, 1], {"mem": other})))
        own_ret[part, 0:CAP, :] = normed[part, spot(me), :]

    parts = []
    for part in range(PARTS):
        for side in (0, 1):
            for number in range(1, 7):
                there = ret.at[side, part, pl.ds(number * CAP, CAP), :]
                sems = (ret_send.at[0, 0], ret_recv.at[side, number, part])
                rcopy(there, there, *sems, {"mem": other}).wait_recv()
            rows = ret[side, part]
            result = jnp.dot(gates[side, 0], rows, preferred_element_type=F32)
            result = result + jnp.dot(gates[side, 1], rows, preferred_element_type=F32)
            part_out[side, part] = result.astype(BF16)
            to = {"mem": mem(z - 1 + 2 * side, core)}
            src, dst, sems = part_out.at[side, part], part_in.at[side, part], part_sems.at[side, part]
            parts.append(go(rcopy(src, dst, sems.at[0], sems.at[1], to)))
    for part in range(PARTS):
        back[part].wait_recv()
        rows = own_ret[part]
        result = jnp.dot(own_gates[0], rows, preferred_element_type=F32)
        result = result + jnp.dot(own_gates[1], rows, preferred_element_type=F32)
        for side in (0, 1):
            parts[2 * part + side].wait_recv()
        result = result + part_in[0, part].astype(F32) + part_in[1, part].astype(F32)
        out[:, part * PART : (part + 1) * PART] = result.astype(BF16)
    for copy in sent:
        copy.wait_send()


def on_device(hidden, routes, gate_levels, query_weight, key_weight, value_weight):
    dma = pltpu.SemaphoreType.DMA
    whole = pl.BlockSpec(memory_space=pl.ANY)
    near = pl.BlockSpec(memory_space=pltpu.VMEM)
    return pl.pallas_call(
        kernel,
        out_shape=jax.ShapeDtypeStruct((TOK, HD), BF16),
        in_specs=[whole, near, near, whole, whole, whole],
        out_specs=near,
        scratch_shapes=[
            pltpu.VMEM((3, TOK, D), BF16),
            pltpu.VMEM((3, 2 * MEMS, TOK), F32),
            pltpu.VMEM((ROWS, D), BF16),
            pltpu.VMEM((2, 7 * CAP, D), BF16),
            pltpu.VMEM((2 * CAP, D), BF16),
            pltpu.VMEM((16, 128, HD), BF16),
            pltpu.VMEM((16, 128, HD), BF16),
            pltpu.VMEM((16, 128, HD), BF16),
            pltpu.VMEM((ROWS, HD), BF16),
            pltpu.VMEM((ROWS, HD), BF16),
            pltpu.VMEM((ROWS, HD), BF16),
            pltpu.VMEM((ROWS, D), BF16),
            pltpu.VMEM((4, HD, DK), F32),
            pltpu.VMEM((HD, DK), F32),
            pltpu.VMEM((HD, DK), F32),
            pltpu.VMEM((4, HD, DK), BF16),
            pltpu.VMEM((4, HD, DK), BF16),
            pltpu.VMEM((4, HD, DK), BF16),
            pltpu.VMEM((ROWS, HD), F32),
            pltpu.VMEM((PARTS, ROWS, PART), BF16),
            pltpu.VMEM((2, PARTS, 8 * CAP, PART), BF16),
            pltpu.VMEM((PARTS, 2 * CAP, PART), BF16),
            pltpu.VMEM((2, 2, TOK, 8 * CAP), BF16),
            pltpu.VMEM((2, TOK, 2 * CAP), BF16),
            pltpu.VMEM((2, PARTS, TOK, PART), BF16),
            pltpu.VMEM((2, PARTS, TOK, PART), BF16),
            dma((3, 20)),
            dma((3, 20)),
            dma((2, 2, 2)),
            dma((2, 2)),
            dma((2, 7, 2)),
            dma((MEMS, 2)),
            dma((2,)),
            dma((4,)),
            dma((2,)),
            dma((4, 2, 2, 2)),
            dma((12, PARTS)),
            dma((2, 7, PARTS)),
            dma((PARTS, 2)),
            dma((2, PARTS, 2)),
        ],
        compiler_params=pltpu.CompilerParams(
            collective_id=0, has_side_effects=True, vmem_limit_bytes=58 * 2**20
        ),
        name="memories",
    )(hidden, routes.T, gate_levels.T, query_weight, key_weight, value_weight)


def solution(mesh):
    return jax.shard_map(
        on_device,
        mesh=mesh,
        in_specs=(
            P(("seq", "mem"), None),
            P(("seq", "mem"), None),
            P(("seq", "mem"), None),
            P("seq", None),
            P("mem", "seq", None),
            P("mem", "seq", None),
        ),
        out_specs=P(("seq", "mem"), None),
        check_vma=False,
    )
```

```python
import jax
import jax.numpy as jnp
from jax import lax
from jax.experimental import pallas as pl
from jax.experimental.pallas import tpu as pltpu
from jax.sharding import PartitionSpec as P

D = 2048
HD = 1024
HEADS = 8
DK = 128
TOK = 256
CAP = 64
MEMS = 16
SIDE = 4
RING = 8
ROWS = MEMS * CAP
HALF = HD // 2
PARTS = 4
PART = HD // PARTS
BLOCK = 256
BF16 = jnp.bfloat16
F32 = jnp.float32
MESH = pl.DeviceIdType.MESH


def tiles(total, width, body):
    @pl.loop(0, total // width)
    def _(step):
        body(pl.ds(pl.multiple_of(step * width, width), width))


def weight_stream(whole, own, base, n, x_first, y, x, send_sems, recv_sems):
    f = x_first * x + (1 - x_first) * y
    g = x_first * y + (1 - x_first) * x

    def place(i, j):
        a, b = lax.rem(f + i + SIDE, SIDE), lax.rem(g + j + SIDE, SIDE)
        return x_first * (b * SIDE + a) + (1 - x_first) * (a * SIDE + b)

    def piece(i, j, part=None):
        start, rows = base, n
        if part is not None:
            start, rows = base + part * (n // 2), n // 2
        return whole.at[place(i, j), pl.ds(start, rows), :]

    def send(number, src, dst, i, j):
        return pltpu.make_async_remote_copy(
            src_ref=src,
            dst_ref=dst,
            send_sem=send_sems.at[number],
            recv_sem=recv_sems.at[number],
            device_id={"seq": place(i, j)},
            device_id_type=MESH,
        )

    def relay(number, i, j, part, di, dj):
        return send(number, piece(i, j, part), piece(i, j, part), di, dj)

    first = [send(c, own, piece(0, 0), *to) for c, to in enumerate(((1, 0), (-1, 0), (0, 1), (0, -1)))]
    copies = first + [
        relay(4, -1, 0, 0, 1, 0),
        relay(5, 1, 0, 1, -1, 0),
        relay(6, 0, -1, 0, 0, 1),
        relay(7, 0, 1, 1, 0, -1),
        relay(8, -1, 0, None, 0, 1),
        relay(9, -1, 0, None, 0, -1),
        relay(10, 1, 0, None, 0, 1),
        relay(11, 1, 0, None, 0, -1),
        relay(12, 2, 0, None, 0, 1),
        relay(13, 2, 0, None, 0, -1),
        relay(14, -1, -1, 0, 0, 1),
        relay(15, -1, 1, 1, 0, -1),
        relay(16, 1, -1, 0, 0, 1),
        relay(17, 1, 1, 1, 0, -1),
        relay(18, 2, -1, 0, 0, 1),
        relay(19, 2, 1, 1, 0, -1),
    ]
    return copies


def kernel(
    hid, routes, levels, qw, kw, vw, out,
    raw, tab, rows_in, near_stage, stage, sib_stage, wq, wk, wv, q, k, v, xs,
    block_states, total, entering, before, s_send, s_recv, reads, normed,
    ret, own_ret, gates, own_gates, part_out, part_in,
    w_send, w_recv, raw_sems, tab_sems, near_send, set_send, set_recv, sib_send, local_sems, swap_sems,
    state_sems, ret_send, ret_recv, own_ret_sems, part_sems,
):
    me, group = lax.axis_index("mem"), lax.axis_index("seq")
    z, core = me // 2, me % 2
    y, x = group // SIDE, group % SIDE

    def mem(chip, c):
        return lax.rem(chip + RING, RING) * 2 + c

    def rcopy(src, dst, send_sem, recv_sem, device):
        return pltpu.make_async_remote_copy(
            src_ref=src, dst_ref=dst, send_sem=send_sem, recv_sem=recv_sem, device_id=device, device_id_type=MESH
        )

    def spot(source):
        return pl.ds(pl.multiple_of(source * CAP, CAP), CAP)

    def columns(part):
        return pl.ds(part * HD, HD)

    sent = []

    def go(copy):
        copy.start()
        sent.append(copy)
        return copy

    other = mem(z, 1 - core)
    barrier = pltpu.get_barrier_semaphore()
    peers = [{"mem": other}]
    peers += [{"mem": mem(z - 1, core)}, {"mem": mem(z + 1, core)}]
    for dx, dy in ((1, 0), (3, 0), (0, 1), (0, 3)):
        peers.append({"seq": lax.rem(y + dy, SIDE) * SIDE + lax.rem(x + dx, SIDE)})
    for peer in peers:
        pl.semaphore_signal(barrier, inc=1, device_id=peer, device_id_type=MESH)

    mine = [
        pltpu.make_async_copy(hid, raw.at[2], local_sems.at[0]),
        pltpu.make_async_copy(kw.at[0], wk.at[group], local_sems.at[1]),
        pltpu.make_async_copy(vw.at[0], wv.at[group], local_sems.at[2]),
    ]
    half = pl.multiple_of(core * CAP, CAP)
    mine.append(
        pltpu.make_async_copy(qw.at[pl.ds(half, CAP), :], wq.at[group, pl.ds(half, CAP), :], local_sems.at[3])
    )
    for copy in mine:
        copy.start()
    ids = lax.broadcasted_iota(jnp.int32, (MEMS, TOK), 0)
    hit0, hit1 = routes[0:1, :] == ids, routes[1:2, :] == ids
    earlier = lax.broadcasted_iota(jnp.int32, (TOK, TOK), 0) < lax.broadcasted_iota(jnp.int32, (TOK, TOK), 1)
    hits = jnp.where(hit0 | hit1, 1.0, 0.0)
    place = jnp.dot(hits.astype(BF16), jnp.where(earlier, 1.0, 0.0).astype(BF16), preferred_element_type=F32)
    lev0, lev1 = levels[0:1, :].astype(F32), levels[1:2, :].astype(F32)
    both = lev0 + lev1
    tab[2, 0:MEMS, :] = jnp.where(hits > 0, place, -1.0)
    tab[2, MEMS : 2 * MEMS, :] = jnp.where(hit0, lev0 / both, 0.0) + jnp.where(hit1, lev1 / both, 0.0)

    pl.semaphore_wait(barrier, len(peers))

    raws, tabs = [], []

    def pass_tables(hop):
        for side, step in ((0, 1), (1, -1)):
            src = tab.at[2] if hop == 0 else tab.at[side]
            sems, to = tab_sems.at[hop, side], {"mem": mem(z + step, core)}
            tabs.append(go(rcopy(src, tab.at[side + 3 * hop], sems.at[0], sems.at[1], to)))

    def pass_rows(hop, part):
        for side, step in ((0, 1), (1, -1)):
            cols, sems = columns(part), raw_sems.at[hop, side, part]
            src = hid.at[:, cols] if hop == 0 else raw.at[side, :, cols]
            to = {"mem": mem(z + step, core)}
            raws.append(go(rcopy(src, raw.at[side + 3 * hop, :, cols], sems.at[0], sems.at[1], to)))

    pass_tables(0)
    pass_rows(0, 0)
    pass_rows(0, 1)
    own_q = qw.at[pl.ds(half, CAP), :]
    keyed = [
        weight_stream(wk, kw.at[0], 0, 128, 1, y, x, w_send.at[0], w_recv.at[0]),
        weight_stream(wv, vw.at[0], 0, 128, 0, y, x, w_send.at[1], w_recv.at[1]),
    ]
    asked = [weight_stream(wq, own_q, half, CAP, 1 - core, y, x, w_send.at[2], w_recv.at[2])]

    def start(streams, *numbers):
        for number in numbers:
            for copies in streams:
                go(copies[number])

    def arrive(streams, *numbers):
        for number in numbers:
            for copies in streams:
                copies[number].wait_recv()

    start(keyed, 0, 1, 2, 3)

    slot = lax.broadcasted_iota(jnp.int32, (CAP, TOK), 0).astype(F32)

    def matches(index, mems):
        return [slot == tab[index, pl.ds(e, 1), :] for e in mems]

    def chosen(index, mems):
        ones = [jnp.where(m, 1.0, 0.0).astype(BF16) for m in matches(index, mems)]
        return jnp.concatenate(ones, axis=0)

    def pack(index, ones, dest, part):
        def body(cols):
            cols = pl.ds(part * HD + cols.start, cols.size)
            dest[:, cols] = jnp.dot(ones, raw[index, :, cols], preferred_element_type=F32).astype(BF16)

        tiles(HD, 512, body)

    def mixing(index, mems, dest, width):
        parts = [
            jnp.where(m, tab[index, pl.ds(MEMS + e, 1), :], 0.0) for m, e in zip(matches(index, mems), mems)
        ]
        if width > len(mems) * CAP:
            parts.append(jnp.zeros((width - len(mems) * CAP, TOK), F32))
        weights = jnp.concatenate(parts, axis=0).T
        high = weights.astype(BF16)
        dest[0] = high
        dest[1] = (weights - high.astype(F32)).astype(BF16)

    def served(side):
        step = 1 - 2 * side
        return [
            me, other,
            mem(z + step, 0), mem(z + step, 1),
            mem(z + 2 * step, 0), mem(z + 2 * step, 1),
            mem(z + 3 * step, side),
        ]

    for copy in mine:
        copy.wait()
    for part in (0, 1):
        pack(2, chosen(2, [me, other]), sib_stage, part)
    for part in (0, 1):
        cols = columns(part)
        src, dst = sib_stage.at[pl.ds(CAP, CAP), cols], rows_in.at[spot(me), cols]
        go(rcopy(src, dst, sib_send.at[part], set_recv.at[me, part], {"mem": other}))
    rows_in[spot(me), :] = sib_stage[0:CAP, :]
    mixing(2, [me, other], own_gates, 2 * CAP)

    arrive(keyed, 0, 1, 2, 3)
    start(keyed, 8, 9, 10, 11, 4, 5, 6, 7)
    start(asked, 0, 1, 2, 3)

    for side in (0, 1):
        tabs[side].wait_recv()
    pass_tables(1)
    for part in (0, 1):
        cols = columns(part)
        for side in (0, 1):
            raws[2 * part + side].wait_recv()
        pass_rows(1, part)
        for side in (0, 1):
            origin = mem(z - 1 + 2 * side, core)
            pack(side, chosen(side, [me, other]), near_stage.at[side], part)
            src, dst = near_stage.at[side, pl.ds(CAP, CAP), cols], rows_in.at[spot(origin), cols]
            go(rcopy(src, dst, near_send.at[side, part], set_recv.at[origin, part], {"mem": other}))
            rows_in[spot(origin), cols] = near_stage[side, 0:CAP, cols]

    def await_rows(sources):
        for source in sources:
            for part in (0, 1):
                there = rows_in.at[spot(source), columns(part)]
                rcopy(there, there, sib_send.at[part], set_recv.at[source, part], {"mem": other}).wait_recv()

    arrive(keyed, 4, 5, 8, 9, 10, 11)
    start(keyed, 12, 13, 14, 15, 16, 17)
    arrive(asked, 0, 1, 2, 3)
    start(asked, 8, 9, 10, 11, 4, 5, 6, 7)
    await_rows([other, mem(z - 1, 1 - core), mem(z + 1, 1 - core)])

    def further(side):
        step = 1 - 2 * side
        return [me, other, mem(z + step, 0), mem(z + step, 1), mem(z + 2 * step, side)]

    for side in (0, 1):
        tabs[2 + side].wait_recv()
    for part in (0, 1):
        for side in (0, 1):
            origin = mem(z - 2 + 4 * side, core)
            mems = further(side)
            cols = columns(part)
            raws[4 + 2 * part + side].wait_recv()
            pack(3 + side, chosen(3 + side, mems), stage.at[side], part)
            for number in (2, 3, 4, 1):
                src, dst = stage.at[side, pl.ds(number * CAP, CAP), cols], rows_in.at[spot(origin), cols]
                sems = (set_send.at[side, number, part], set_recv.at[origin, part])
                go(rcopy(src, dst, *sems, {"mem": mems[number]}))
            rows_in[spot(origin), cols] = stage[side, 0:CAP, cols]
        if part == 0:
            arrive(keyed, 12, 13)
            start(keyed, 18, 19)
            arrive(asked, 4, 5, 8, 9, 10, 11)
            start(asked, 12, 13, 14, 15, 16, 17)

    for side in (0, 1):
        mixing(side, served(side), gates.at[side], 8 * CAP)
        ret[side, :, 7 * CAP : 8 * CAP, :] = jnp.zeros((PARTS, CAP, PART), BF16)
    arrive(keyed, 6, 7, 14, 15, 16, 17, 18, 19)

    def take(first, sources):
        for n, source in enumerate(sources):
            xs[first + n * CAP : first + (n + 1) * CAP, :] = rows_in[spot(source), :]

    def project(first, sources, weight, dest):
        many = len(sources) * CAP
        width = HD if many <= 384 else HALF

        def body(cols):
            w = weight[:, :, cols].reshape(D, width)
            result = jnp.dot(xs[first : first + many, :], w, preferred_element_type=F32).astype(BF16)
            for n, source in enumerate(sources):
                dest[spot(source), cols] = result[n * CAP : (n + 1) * CAP]

        tiles(HD, width, body)

    causal = lax.broadcasted_iota(jnp.int32, (BLOCK, BLOCK), 0) >= lax.broadcasted_iota(
        jnp.int32, (BLOCK, BLOCK), 1
    )
    first_block = lax.rem((z + 1) // 2 + 3, 4)
    turn = [lax.rem(first_block + n, 4) for n in range(4)]

    def head_cols(h):
        return pl.ds(pl.multiple_of(h * DK, DK), DK)

    def state_rows(h):
        return pl.ds(pl.multiple_of((lax.rem(h, 2) * (HEADS // 2) + h // 2) * DK, DK), DK)

    def attend(blocks, h):
        cols = head_cols(h)
        for b in blocks:
            rows = pl.ds(pl.multiple_of(b * BLOCK, BLOCK), BLOCK)
            scores = lax.dot_general(
                q[rows, cols], k[rows, cols], (((1,), (1,)), ((), ())), preferred_element_type=F32
            )
            scores = jnp.where(causal, scores, 0.0).astype(BF16)
            reads[rows, cols] = jnp.dot(scores, v[rows, cols], preferred_element_type=F32)

    def add_up(blocks, h):
        cols = head_cols(h)
        for b in blocks:
            rows = pl.ds(pl.multiple_of(b * BLOCK, BLOCK), BLOCK)
            block_states[b, state_rows(h), :] = lax.dot_general(
                k[rows, cols], v[rows, cols], (((0,), (0,)), ((), ())), preferred_element_type=F32
            )

    near = [me, other] + [mem(z + d, c) for d in (-1, 1) for c in (core, 1 - core)]
    take(0, near)
    project(0, near, wk, k)
    arrive(asked, 12, 13)
    start(asked, 18, 19)
    project(0, near, wv, v)
    arrive(asked, 6, 7, 14, 15, 16, 17, 18, 19)
    halves = wq.at[:, pl.ds(half, CAP), :]
    swap = go(rcopy(halves, halves, swap_sems.at[0], swap_sems.at[1], {"mem": other}))
    middle = [mem(z + d, c) for d in (-2, 2) for c in (0, 1)]
    await_rows([mem(z + d, 1 - core) for d in (-2, 2)])
    take(384, middle)
    project(384, middle, wk, k)
    project(384, middle, wv, v)

    @pl.loop(0, HEADS)
    def _(h):
        add_up(turn[:2], h)

    far = [mem(z + d, c) for d in (-3, 3) for c in (0, 1)]
    await_rows(far)
    take(640, far)
    project(640, far, wk, k)
    project(640, far, wv, v)
    swap.wait_recv()
    project(0, near + middle + far, wq, q)
    last_ones = [mem(z + 4, c) for c in (0, 1)]
    await_rows(last_ones)
    take(896, last_ones)
    project(896, last_ones, wk, k)
    project(896, last_ones, wv, v)

    @pl.loop(0, HEADS)
    def _(h):
        add_up(turn[2:], h)
        rows = state_rows(h)
        total[rows, :] = (block_states[0, rows, :] + block_states[1, rows, :]) + (
            block_states[2, rows, :] + block_states[3, rows, :]
        )

    def at(row, column):
        return row * SIDE + column

    y1, y3 = y + 1 - 2 * (y % 2), SIDE - 1 - y
    x1, x3 = x + 1 - 2 * (x % 2), SIDE - 1 - x
    sums = [(at(y, x1), x % 2), (at(y, x3), x // 2), (at(y1, x), y % 2), (at(y3, x), y // 2)]
    befores = [(at(y3, x), 1 - y // 2), (at(y1, x), 1 - y % 2), (at(y, x3), 1 - x // 2), (at(y, x1), 1 - x % 2)]
    entering[...] = jnp.zeros_like(entering)
    moving = {}

    def low_high(pair):
        return pl.ds(pair * PART, PART), pl.ds(HALF + pair * PART, PART)

    def push(step, pair):
        low, high = low_high(pair)
        s_send[step, low, :] = total[low, :].astype(BF16)
        s_send[step, high, :] = (entering[high, :] + total[high, :] * befores[step][1].astype(F32)).astype(BF16)
        for stream, (rows, to) in enumerate(((low, sums[step][0]), (high, befores[step][0]))):
            sems = state_sems.at[step, pair, stream]
            src, dst = s_send.at[step, rows], s_recv.at[step, rows]
            moving[step, pair, stream] = go(rcopy(src, dst, sems.at[0], sems.at[1], {"seq": to}))

    def pull(step, pair):
        low, high = low_high(pair)
        moving[step, pair, 0].wait_recv()
        moving[step, pair, 1].wait_recv()
        theirs = s_recv[step, low, :].astype(F32)
        entering[low, :] += theirs * sums[step][1].astype(F32)
        if step < 3:
            total[low, :] += theirs
        entering[high, :] += s_recv[step, high, :].astype(F32)

    push(0, 0)
    push(0, 1)
    project(896, last_ones, wq, q)
    running = jnp.zeros((HD, DK), F32)
    for b in range(4):
        before[b] = running.astype(BF16)
        running = running + block_states[b]
    for step in range(3):
        for pair in (0, 1):
            for h in ((0, 1), (2,), (3, 4), (5,), (6,), (7,))[2 * step + pair]:
                attend(turn, h)
            pull(step, pair)
            push(step + 1, pair)
    pull(3, 0)

    def finish(chip, part):
        chip = lax.rem(chip + RING, RING)
        rows = pl.ds(pl.multiple_of(chip * 128, 128), 128)
        for h in (2 * part, 2 * part + 1):
            cols = slice(h * DK, (h + 1) * DK)
            place = h % 2 * (HEADS // 2) + h // 2
            states = slice(place * DK, (place + 1) * DK)
            state = (entering[states, :] + before[chip // 2, states, :].astype(F32)).astype(BF16)
            read = reads[rows, cols] + jnp.dot(q[rows, cols], state, preferred_element_type=F32)
            scale = lax.rsqrt(jnp.mean(read * read, axis=1, keepdims=True) + 1e-6)
            normed[part, rows, h % 2 * DK : (h % 2 + 1) * DK] = (read * scale).astype(BF16)

    def give(part, source, node, side, number, sem):
        src, dst = normed.at[part, spot(source)], ret.at[side, part, spot(number)]
        go(rcopy(src, dst, ret_send.at[sem, part], ret_recv.at[side, number, part], {"mem": node}))

    back = []
    for part in range(PARTS):
        if part == 2:
            pull(3, 1)
        finish(z + 4, part)
        for c in (0, 1):
            give(part, mem(z + 4, c), mem(z + 5 - 2 * core, c), core, 6, c)
        sem = 2
        for distance in (3, 2):
            for side in (0, 1):
                step = 1 - 2 * side
                finish(z - distance * step, part)
                for c in (0, 1):
                    source, node = mem(z - distance * step, c), mem(z - (distance - 1) * step, c)
                    give(part, source, node, side, 2 * (distance - 1) + core, sem)
                    sem += 1
        for side in (0, 1):
            chip = z - 1 + 2 * side
            finish(chip, part)
            give(part, mem(chip, 1 - core), other, side, 1, sem)
            sem += 1
            ret[side, part, 0:CAP, :] = normed[part, spot(mem(chip, core)), :]
        finish(z, part)
        src, dst = normed.at[part, spot(other)], own_ret.at[part, pl.ds(CAP, CAP), :]
        back.append(go(rcopy(src, dst, own_ret_sems.at[part, 0], own_ret_sems.at[part, 1], {"mem": other})))
        own_ret[part, 0:CAP, :] = normed[part, spot(me), :]

    parts = []
    for part in range(PARTS):
        for side in (0, 1):
            for number in range(1, 7):
                there = ret.at[side, part, pl.ds(number * CAP, CAP), :]
                sems = (ret_send.at[0, 0], ret_recv.at[side, number, part])
                rcopy(there, there, *sems, {"mem": other}).wait_recv()
            rows = ret[side, part]
            result = jnp.dot(gates[side, 0], rows, preferred_element_type=F32)
            result = result + jnp.dot(gates[side, 1], rows, preferred_element_type=F32)
            part_out[side, part] = result.astype(BF16)
            to = {"mem": mem(z - 1 + 2 * side, core)}
            src, dst, sems = part_out.at[side, part], part_in.at[side, part], part_sems.at[side, part]
            parts.append(go(rcopy(src, dst, sems.at[0], sems.at[1], to)))
    for part in range(PARTS):
        back[part].wait_recv()
        rows = own_ret[part]
        result = jnp.dot(own_gates[0], rows, preferred_element_type=F32)
        result = result + jnp.dot(own_gates[1], rows, preferred_element_type=F32)
        for side in (0, 1):
            parts[2 * part + side].wait_recv()
        result = result + part_in[0, part].astype(F32) + part_in[1, part].astype(F32)
        out[:, part * PART : (part + 1) * PART] = result.astype(BF16)
    for copy in sent:
        copy.wait_send()


def on_device(hidden, routes, gate_levels, query_weight, key_weight, value_weight):
    dma = pltpu.SemaphoreType.DMA
    whole = pl.BlockSpec(memory_space=pl.ANY)
    near = pl.BlockSpec(memory_space=pltpu.VMEM)
    return pl.pallas_call(
        kernel,
        out_shape=jax.ShapeDtypeStruct((TOK, HD), BF16),
        in_specs=[whole, near, near, whole, whole, whole],
        out_specs=near,
        scratch_shapes=[
            pltpu.VMEM((5, TOK, D), BF16),
            pltpu.VMEM((5, 2 * MEMS, TOK), F32),
            pltpu.VMEM((ROWS, D), BF16),
            pltpu.VMEM((2, 2 * CAP, D), BF16),
            pltpu.VMEM((2, 5 * CAP, D), BF16),
            pltpu.VMEM((2 * CAP, D), BF16),
            pltpu.VMEM((16, 128, HD), BF16),
            pltpu.VMEM((16, 128, HD), BF16),
            pltpu.VMEM((16, 128, HD), BF16),
            pltpu.VMEM((ROWS, HD), BF16),
            pltpu.VMEM((ROWS, HD), BF16),
            pltpu.VMEM((ROWS, HD), BF16),
            pltpu.VMEM((ROWS, D), BF16),
            pltpu.VMEM((4, HD, DK), F32),
            pltpu.VMEM((HD, DK), F32),
            pltpu.VMEM((HD, DK), F32),
            pltpu.VMEM((4, HD, DK), BF16),
            pltpu.VMEM((4, HD, DK), BF16),
            pltpu.VMEM((4, HD, DK), BF16),
            pltpu.VMEM((ROWS, HD), F32),
            pltpu.VMEM((PARTS, ROWS, PART), BF16),
            pltpu.VMEM((2, PARTS, 8 * CAP, PART), BF16),
            pltpu.VMEM((PARTS, 2 * CAP, PART), BF16),
            pltpu.VMEM((2, 2, TOK, 8 * CAP), BF16),
            pltpu.VMEM((2, TOK, 2 * CAP), BF16),
            pltpu.VMEM((2, PARTS, TOK, PART), BF16),
            pltpu.VMEM((2, PARTS, TOK, PART), BF16),
            dma((3, 20)),
            dma((3, 20)),
            dma((2, 2, 2, 2)),
            dma((2, 2, 2)),
            dma((2, 2)),
            dma((2, 5, 2)),
            dma((MEMS, 2)),
            dma((2,)),
            dma((4,)),
            dma((2,)),
            dma((4, 2, 2, 2)),
            dma((12, PARTS)),
            dma((2, 7, PARTS)),
            dma((PARTS, 2)),
            dma((2, PARTS, 2)),
        ],
        compiler_params=pltpu.CompilerParams(
            collective_id=0, has_side_effects=True, vmem_limit_bytes=58 * 2**20
        ),
        name="memories",
    )(hidden, routes.T, gate_levels.T, query_weight, key_weight, value_weight)


def solution(mesh):
    return jax.shard_map(
        on_device,
        mesh=mesh,
        in_specs=(
            P(("seq", "mem"), None),
            P(("seq", "mem"), None),
            P(("seq", "mem"), None),
            P("seq", None),
            P("mem", "seq", None),
            P("mem", "seq", None),
        ),
        out_specs=P(("seq", "mem"), None),
        check_vma=False,
    )
```

```python
import jax
import jax.numpy as jnp
from jax import lax
from jax.experimental import pallas as pl
from jax.experimental.pallas import tpu as pltpu
from jax.sharding import PartitionSpec as P

D = 2048
HD = 1024
HEADS = 8
DK = 128
TOK = 256
CAP = 64
MEMS = 16
SIDE = 4
RING = 8
ROWS = MEMS * CAP
HALF = HD // 2
PARTS = 4
PART = HD // PARTS
BLOCK = 256
BF16 = jnp.bfloat16
F32 = jnp.float32
MESH = pl.DeviceIdType.MESH


def tiles(total, width, body):
    @pl.loop(0, total // width)
    def _(step):
        body(pl.ds(pl.multiple_of(step * width, width), width))


def weight_stream(whole, own, base, n, x_first, y, x, send_sems, recv_sems):
    f = x_first * x + (1 - x_first) * y
    g = x_first * y + (1 - x_first) * x

    def place(i, j):
        a, b = lax.rem(f + i + SIDE, SIDE), lax.rem(g + j + SIDE, SIDE)
        return x_first * (b * SIDE + a) + (1 - x_first) * (a * SIDE + b)

    def piece(i, j, part=None):
        start, rows = base, n
        if part is not None:
            start, rows = base + part * (n // 2), n // 2
        return whole.at[place(i, j), pl.ds(start, rows), :]

    def send(number, src, dst, i, j):
        return pltpu.make_async_remote_copy(
            src_ref=src,
            dst_ref=dst,
            send_sem=send_sems.at[number],
            recv_sem=recv_sems.at[number],
            device_id={"seq": place(i, j)},
            device_id_type=MESH,
        )

    def relay(number, i, j, part, di, dj):
        return send(number, piece(i, j, part), piece(i, j, part), di, dj)

    first = [send(c, own, piece(0, 0), *to) for c, to in enumerate(((1, 0), (-1, 0), (0, 1), (0, -1)))]
    copies = first + [
        relay(4, -1, 0, 0, 1, 0),
        relay(5, 1, 0, 1, -1, 0),
        relay(6, 0, -1, 0, 0, 1),
        relay(7, 0, 1, 1, 0, -1),
        relay(8, -1, 0, None, 0, 1),
        relay(9, -1, 0, None, 0, -1),
        relay(10, 1, 0, None, 0, 1),
        relay(11, 1, 0, None, 0, -1),
        relay(12, 2, 0, None, 0, 1),
        relay(13, 2, 0, None, 0, -1),
        relay(14, -1, -1, 0, 0, 1),
        relay(15, -1, 1, 1, 0, -1),
        relay(16, 1, -1, 0, 0, 1),
        relay(17, 1, 1, 1, 0, -1),
        relay(18, 2, -1, 0, 0, 1),
        relay(19, 2, 1, 1, 0, -1),
    ]
    return copies


def kernel(
    hid, routes, levels, qw, kw, vw, out,
    raw, tab, rows_in, near_stage, stage, sib_stage, wq, wk, wv, q, k, v, xs,
    block_states, total, entering, before, s_send, s_recv, reads, normed,
    ret, own_ret, gates, own_gates, part_out, part_in,
    w_send, w_recv, raw_sems, tab_sems, near_send, set_send, set_recv, sib_send, local_sems, swap_sems,
    state_sems, ret_send, ret_recv, own_ret_sems, part_sems,
):
    me, group = lax.axis_index("mem"), lax.axis_index("seq")
    z, core = me // 2, me % 2
    y, x = group // SIDE, group % SIDE

    def mem(chip, c):
        return lax.rem(chip + RING, RING) * 2 + c

    def rcopy(src, dst, send_sem, recv_sem, device):
        return pltpu.make_async_remote_copy(
            src_ref=src, dst_ref=dst, send_sem=send_sem, recv_sem=recv_sem, device_id=device, device_id_type=MESH
        )

    def spot(source):
        return pl.ds(pl.multiple_of(source * CAP, CAP), CAP)

    def columns(part):
        return pl.ds(part * HD, HD)

    sent = []

    def go(copy):
        copy.start()
        sent.append(copy)
        return copy

    other = mem(z, 1 - core)
    barrier = pltpu.get_barrier_semaphore()
    peers = [{"mem": other}]
    peers += [{"mem": mem(z - 1, core)}, {"mem": mem(z + 1, core)}]
    for dx, dy in ((1, 0), (3, 0), (0, 1), (0, 3)):
        peers.append({"seq": lax.rem(y + dy, SIDE) * SIDE + lax.rem(x + dx, SIDE)})
    for peer in peers:
        pl.semaphore_signal(barrier, inc=1, device_id=peer, device_id_type=MESH)

    mine = [
        pltpu.make_async_copy(hid, raw.at[2], local_sems.at[0]),
        pltpu.make_async_copy(kw.at[0], wk.at[group], local_sems.at[1]),
        pltpu.make_async_copy(vw.at[0], wv.at[group], local_sems.at[2]),
    ]
    half = pl.multiple_of(core * CAP, CAP)
    mine.append(
        pltpu.make_async_copy(qw.at[pl.ds(half, CAP), :], wq.at[group, pl.ds(half, CAP), :], local_sems.at[3])
    )
    for copy in mine:
        copy.start()
    ids = lax.broadcasted_iota(jnp.int32, (MEMS, TOK), 0)
    hit0, hit1 = routes[0:1, :] == ids, routes[1:2, :] == ids
    earlier = lax.broadcasted_iota(jnp.int32, (TOK, TOK), 0) < lax.broadcasted_iota(jnp.int32, (TOK, TOK), 1)
    hits = jnp.where(hit0 | hit1, 1.0, 0.0)
    place = jnp.dot(hits.astype(BF16), jnp.where(earlier, 1.0, 0.0).astype(BF16), preferred_element_type=F32)
    lev0, lev1 = levels[0:1, :].astype(F32), levels[1:2, :].astype(F32)
    both = lev0 + lev1
    tab[2, 0:MEMS, :] = jnp.where(hits > 0, place, -1.0)
    tab[2, MEMS : 2 * MEMS, :] = jnp.where(hit0, lev0 / both, 0.0) + jnp.where(hit1, lev1 / both, 0.0)

    pl.semaphore_wait(barrier, len(peers))

    raws, tabs = [], []

    def pass_tables(hop):
        for side, step in ((0, 1), (1, -1)):
            src = tab.at[2] if hop == 0 else tab.at[side]
            sems, to = tab_sems.at[hop, side], {"mem": mem(z + step, core)}
            tabs.append(go(rcopy(src, tab.at[side + 3 * hop], sems.at[0], sems.at[1], to)))

    def pass_rows(hop, part):
        for side, step in ((0, 1), (1, -1)):
            cols, sems = columns(part), raw_sems.at[hop, side, part]
            src = hid.at[:, cols] if hop == 0 else raw.at[side, :, cols]
            to = {"mem": mem(z + step, core)}
            raws.append(go(rcopy(src, raw.at[side + 3 * hop, :, cols], sems.at[0], sems.at[1], to)))

    pass_tables(0)
    pass_rows(0, 0)
    pass_rows(0, 1)
    own_q = qw.at[pl.ds(half, CAP), :]
    keyed = [
        weight_stream(wk, kw.at[0], 0, 128, 1, y, x, w_send.at[0], w_recv.at[0]),
        weight_stream(wv, vw.at[0], 0, 128, 0, y, x, w_send.at[1], w_recv.at[1]),
    ]
    asked = [weight_stream(wq, own_q, half, CAP, 1 - core, y, x, w_send.at[2], w_recv.at[2])]

    def start(streams, *numbers):
        for number in numbers:
            for copies in streams:
                go(copies[number])

    def arrive(streams, *numbers):
        for number in numbers:
            for copies in streams:
                copies[number].wait_recv()

    start(keyed, 0, 1, 2, 3)

    slot = lax.broadcasted_iota(jnp.int32, (CAP, TOK), 0).astype(F32)

    def matches(index, mems):
        return [slot == tab[index, pl.ds(e, 1), :] for e in mems]

    def chosen(index, mems):
        ones = [jnp.where(m, 1.0, 0.0).astype(BF16) for m in matches(index, mems)]
        return jnp.concatenate(ones, axis=0)

    def pack(index, ones, dest, part):
        def body(cols):
            cols = pl.ds(part * HD + cols.start, cols.size)
            dest[:, cols] = jnp.dot(ones, raw[index, :, cols], preferred_element_type=F32).astype(BF16)

        tiles(HD, 512, body)

    def mixing(index, mems, dest, width):
        parts = [
            jnp.where(m, tab[index, pl.ds(MEMS + e, 1), :], 0.0) for m, e in zip(matches(index, mems), mems)
        ]
        if width > len(mems) * CAP:
            parts.append(jnp.zeros((width - len(mems) * CAP, TOK), F32))
        weights = jnp.concatenate(parts, axis=0).T
        high = weights.astype(BF16)
        dest[0] = high
        dest[1] = (weights - high.astype(F32)).astype(BF16)

    def served(side):
        step = 1 - 2 * side
        return [
            me, other,
            mem(z + step, 0), mem(z + step, 1),
            mem(z + 2 * step, 0), mem(z + 2 * step, 1),
            mem(z + 3 * step, side),
        ]

    for copy in mine:
        copy.wait()
    for part in (0, 1):
        pack(2, chosen(2, [me, other]), sib_stage, part)
    for part in (0, 1):
        cols = columns(part)
        src, dst = sib_stage.at[pl.ds(CAP, CAP), cols], rows_in.at[spot(me), cols]
        go(rcopy(src, dst, sib_send.at[part], set_recv.at[me, part], {"mem": other}))
    rows_in[spot(me), :] = sib_stage[0:CAP, :]
    mixing(2, [me, other], own_gates, 2 * CAP)

    arrive(keyed, 0, 1, 2, 3)
    start(keyed, 8, 9, 10, 11, 4, 5, 6, 7)
    start(asked, 0, 1, 2, 3)

    for side in (0, 1):
        tabs[side].wait_recv()
    pass_tables(1)
    for part in (0, 1):
        cols = columns(part)
        for side in (0, 1):
            raws[2 * part + side].wait_recv()
        pass_rows(1, part)
        for side in (0, 1):
            origin = mem(z - 1 + 2 * side, core)
            pack(side, chosen(side, [me, other]), near_stage.at[side], part)
            src, dst = near_stage.at[side, pl.ds(CAP, CAP), cols], rows_in.at[spot(origin), cols]
            go(rcopy(src, dst, near_send.at[side, part], set_recv.at[origin, part], {"mem": other}))
            rows_in[spot(origin), cols] = near_stage[side, 0:CAP, cols]

    def await_rows(sources):
        for source in sources:
            for part in (0, 1):
                there = rows_in.at[spot(source), columns(part)]
                rcopy(there, there, sib_send.at[part], set_recv.at[source, part], {"mem": other}).wait_recv()

    arrive(keyed, 4, 5, 8, 9, 10, 11)
    start(keyed, 12, 13, 14, 15, 16, 17)
    arrive(asked, 0, 1, 2, 3)
    start(asked, 8, 9, 10, 11, 4, 5, 6, 7)
    await_rows([other, mem(z - 1, 1 - core), mem(z + 1, 1 - core)])

    def further(side):
        step = 1 - 2 * side
        return [me, other, mem(z + step, 0), mem(z + step, 1), mem(z + 2 * step, side)]

    for side in (0, 1):
        tabs[2 + side].wait_recv()
    for part in (0, 1):
        for side in (0, 1):
            origin = mem(z - 2 + 4 * side, core)
            mems = further(side)
            cols = columns(part)
            raws[4 + 2 * part + side].wait_recv()
            pack(3 + side, chosen(3 + side, mems), stage.at[side], part)
            for number in (2, 3, 4, 1):
                src, dst = stage.at[side, pl.ds(number * CAP, CAP), cols], rows_in.at[spot(origin), cols]
                sems = (set_send.at[side, number, part], set_recv.at[origin, part])
                go(rcopy(src, dst, *sems, {"mem": mems[number]}))
            rows_in[spot(origin), cols] = stage[side, 0:CAP, cols]
        if part == 0:
            arrive(keyed, 12, 13)
            start(keyed, 18, 19)
            arrive(asked, 4, 5, 8, 9, 10, 11)
            start(asked, 12, 13, 14, 15, 16, 17)

    for side in (0, 1):
        mixing(side, served(side), gates.at[side], 8 * CAP)
        ret[side, :, 7 * CAP : 8 * CAP, :] = jnp.zeros((PARTS, CAP, PART), BF16)
    arrive(keyed, 6, 7, 14, 15, 16, 17, 18, 19)

    def take(first, sources):
        for n, source in enumerate(sources):
            xs[first + n * CAP : first + (n + 1) * CAP, :] = rows_in[spot(source), :]

    def project(first, sources, weight, dest):
        many = len(sources) * CAP
        width = HD if many <= 384 else HALF

        def body(cols):
            w = weight[:, :, cols].reshape(D, width)
            result = jnp.dot(xs[first : first + many, :], w, preferred_element_type=F32).astype(BF16)
            for n, source in enumerate(sources):
                dest[spot(source), cols] = result[n * CAP : (n + 1) * CAP]

        tiles(HD, width, body)

    causal = lax.broadcasted_iota(jnp.int32, (BLOCK, BLOCK), 0) >= lax.broadcasted_iota(
        jnp.int32, (BLOCK, BLOCK), 1
    )
    first_block = lax.rem((z + 1) // 2 + 3, 4)
    turn = [lax.rem(first_block + n, 4) for n in range(4)]

    def head_cols(h):
        return pl.ds(pl.multiple_of(h * DK, DK), DK)

    def state_rows(h):
        return pl.ds(pl.multiple_of((lax.rem(h, 2) * (HEADS // 2) + h // 2) * DK, DK), DK)

    def attend(blocks, h):
        cols = head_cols(h)
        for b in blocks:
            rows = pl.ds(pl.multiple_of(b * BLOCK, BLOCK), BLOCK)
            scores = lax.dot_general(
                q[rows, cols], k[rows, cols], (((1,), (1,)), ((), ())), preferred_element_type=F32
            )
            scores = jnp.where(causal, scores, 0.0).astype(BF16)
            reads[rows, cols] = jnp.dot(scores, v[rows, cols], preferred_element_type=F32)

    def add_up(blocks, h):
        cols = head_cols(h)
        for b in blocks:
            rows = pl.ds(pl.multiple_of(b * BLOCK, BLOCK), BLOCK)
            block_states[b, state_rows(h), :] = lax.dot_general(
                k[rows, cols], v[rows, cols], (((0,), (0,)), ((), ())), preferred_element_type=F32
            )

    near = [me, other] + [mem(z + d, c) for d in (-1, 1) for c in (core, 1 - core)]
    take(0, near)
    project(0, near, wk, k)
    arrive(asked, 12, 13)
    start(asked, 18, 19)
    project(0, near, wv, v)
    arrive(asked, 6, 7, 14, 15, 16, 17, 18, 19)
    halves = wq.at[:, pl.ds(half, CAP), :]
    swap = go(rcopy(halves, halves, swap_sems.at[0], swap_sems.at[1], {"mem": other}))
    middle = [mem(z + d, c) for d in (-2, 2) for c in (0, 1)]
    await_rows([mem(z + d, 1 - core) for d in (-2, 2)])
    take(384, middle)
    project(384, middle, wk, k)
    project(384, middle, wv, v)

    @pl.loop(0, HEADS)
    def _(h):
        add_up(turn[:2], h)

    far = [mem(z + d, c) for d in (-3, 3) for c in (0, 1)]
    swap.wait_recv()
    project(0, near + middle, wq, q)

    @pl.loop(0, HEADS // 2)
    def _(h):
        attend(turn[:2], h)

    await_rows(far)
    take(640, far)
    project(640, far, wk, k)
    project(640, far, wv, v)
    last_ones = [mem(z + 4, c) for c in (0, 1)]
    await_rows(last_ones)
    take(896, last_ones)
    project(896, last_ones, wk, k)
    project(896, last_ones, wv, v)

    def at(row, column):
        return row * SIDE + column

    y1, y3 = y + 1 - 2 * (y % 2), SIDE - 1 - y
    x1, x3 = x + 1 - 2 * (x % 2), SIDE - 1 - x
    sums = [(at(y, x1), x % 2), (at(y, x3), x // 2), (at(y1, x), y % 2), (at(y3, x), y // 2)]
    befores = [(at(y3, x), 1 - y // 2), (at(y1, x), 1 - y % 2), (at(y, x3), 1 - x // 2), (at(y, x1), 1 - x % 2)]
    entering[...] = jnp.zeros_like(entering)
    moving = {}

    def low_high(pair):
        return pl.ds(pair * DK, DK), pl.ds(HALF + pair * DK, DK)

    def push(step, pair):
        low, high = low_high(pair)
        s_send[step, low, :] = total[low, :].astype(BF16)
        s_send[step, high, :] = (entering[high, :] + total[high, :] * befores[step][1].astype(F32)).astype(BF16)
        for stream, (rows, to) in enumerate(((low, sums[step][0]), (high, befores[step][0]))):
            sems = state_sems.at[step, pair, stream]
            src, dst = s_send.at[step, rows], s_recv.at[step, rows]
            moving[step, pair, stream] = go(rcopy(src, dst, sems.at[0], sems.at[1], {"seq": to}))

    def pull(step, pair):
        low, high = low_high(pair)
        moving[step, pair, 0].wait_recv()
        moving[step, pair, 1].wait_recv()
        theirs = s_recv[step, low, :].astype(F32)
        entering[low, :] += theirs * sums[step][1].astype(F32)
        if step < 3:
            total[low, :] += theirs
        entering[high, :] += s_recv[step, high, :].astype(F32)

    for pair in range(PARTS):
        for h in (2 * pair, 2 * pair + 1):
            add_up(turn[2:], h)
        for rows in low_high(pair):
            total[rows, :] = (block_states[0, rows, :] + block_states[1, rows, :]) + (
                block_states[2, rows, :] + block_states[3, rows, :]
            )
        push(0, pair)
    project(640, far + last_ones, wq, q)
    running = jnp.zeros((HD, DK), F32)
    for b in range(4):
        before[b] = running.astype(BF16)
        running = running + block_states[b]
    tasks = [(turn[2:], h) for h in range(HEADS)] + [(turn[:2], h) for h in range(HEADS // 2, HEADS)]
    for step in range(3):
        for pair in range(PARTS):
            attend(*tasks[step * PARTS + pair])
            pull(step, pair)
            push(step + 1, pair)

    def finish(chip, part):
        chip = lax.rem(chip + RING, RING)
        rows = pl.ds(pl.multiple_of(chip * 128, 128), 128)
        for h in (2 * part, 2 * part + 1):
            cols = slice(h * DK, (h + 1) * DK)
            place = h % 2 * (HEADS // 2) + h // 2
            states = slice(place * DK, (place + 1) * DK)
            state = (entering[states, :] + before[chip // 2, states, :].astype(F32)).astype(BF16)
            read = reads[rows, cols] + jnp.dot(q[rows, cols], state, preferred_element_type=F32)
            scale = lax.rsqrt(jnp.mean(read * read, axis=1, keepdims=True) + 1e-6)
            normed[part, rows, h % 2 * DK : (h % 2 + 1) * DK] = (read * scale).astype(BF16)

    def give(part, source, node, side, number, sem):
        src, dst = normed.at[part, spot(source)], ret.at[side, part, spot(number)]
        go(rcopy(src, dst, ret_send.at[sem, part], ret_recv.at[side, number, part], {"mem": node}))

    back = []
    for part in range(PARTS):
        pull(3, part)
        finish(z + 4, part)
        for c in (0, 1):
            give(part, mem(z + 4, c), mem(z + 5 - 2 * core, c), core, 6, c)
        sem = 2
        for distance in (3, 2):
            for side in (0, 1):
                step = 1 - 2 * side
                finish(z - distance * step, part)
                for c in (0, 1):
                    source, node = mem(z - distance * step, c), mem(z - (distance - 1) * step, c)
                    give(part, source, node, side, 2 * (distance - 1) + core, sem)
                    sem += 1
        for side in (0, 1):
            chip = z - 1 + 2 * side
            finish(chip, part)
            give(part, mem(chip, 1 - core), other, side, 1, sem)
            sem += 1
            ret[side, part, 0:CAP, :] = normed[part, spot(mem(chip, core)), :]
        finish(z, part)
        src, dst = normed.at[part, spot(other)], own_ret.at[part, pl.ds(CAP, CAP), :]
        back.append(go(rcopy(src, dst, own_ret_sems.at[part, 0], own_ret_sems.at[part, 1], {"mem": other})))
        own_ret[part, 0:CAP, :] = normed[part, spot(me), :]

    parts = []
    for part in range(PARTS):
        for side in (0, 1):
            for number in range(1, 7):
                there = ret.at[side, part, pl.ds(number * CAP, CAP), :]
                sems = (ret_send.at[0, 0], ret_recv.at[side, number, part])
                rcopy(there, there, *sems, {"mem": other}).wait_recv()
            rows = ret[side, part]
            result = jnp.dot(gates[side, 0], rows, preferred_element_type=F32)
            result = result + jnp.dot(gates[side, 1], rows, preferred_element_type=F32)
            part_out[side, part] = result.astype(BF16)
            to = {"mem": mem(z - 1 + 2 * side, core)}
            src, dst, sems = part_out.at[side, part], part_in.at[side, part], part_sems.at[side, part]
            parts.append(go(rcopy(src, dst, sems.at[0], sems.at[1], to)))
    for part in range(PARTS):
        back[part].wait_recv()
        rows = own_ret[part]
        result = jnp.dot(own_gates[0], rows, preferred_element_type=F32)
        result = result + jnp.dot(own_gates[1], rows, preferred_element_type=F32)
        for side in (0, 1):
            parts[2 * part + side].wait_recv()
        result = result + part_in[0, part].astype(F32) + part_in[1, part].astype(F32)
        out[:, part * PART : (part + 1) * PART] = result.astype(BF16)
    for copy in sent:
        copy.wait_send()


def on_device(hidden, routes, gate_levels, query_weight, key_weight, value_weight):
    dma = pltpu.SemaphoreType.DMA
    whole = pl.BlockSpec(memory_space=pl.ANY)
    near = pl.BlockSpec(memory_space=pltpu.VMEM)
    return pl.pallas_call(
        kernel,
        out_shape=jax.ShapeDtypeStruct((TOK, HD), BF16),
        in_specs=[whole, near, near, whole, whole, whole],
        out_specs=near,
        scratch_shapes=[
            pltpu.VMEM((5, TOK, D), BF16),
            pltpu.VMEM((5, 2 * MEMS, TOK), F32),
            pltpu.VMEM((ROWS, D), BF16),
            pltpu.VMEM((2, 2 * CAP, D), BF16),
            pltpu.VMEM((2, 5 * CAP, D), BF16),
            pltpu.VMEM((2 * CAP, D), BF16),
            pltpu.VMEM((16, 128, HD), BF16),
            pltpu.VMEM((16, 128, HD), BF16),
            pltpu.VMEM((16, 128, HD), BF16),
            pltpu.VMEM((ROWS, HD), BF16),
            pltpu.VMEM((ROWS, HD), BF16),
            pltpu.VMEM((ROWS, HD), BF16),
            pltpu.VMEM((ROWS, D), BF16),
            pltpu.VMEM((4, HD, DK), F32),
            pltpu.VMEM((HD, DK), F32),
            pltpu.VMEM((HD, DK), F32),
            pltpu.VMEM((4, HD, DK), BF16),
            pltpu.VMEM((4, HD, DK), BF16),
            pltpu.VMEM((4, HD, DK), BF16),
            pltpu.VMEM((ROWS, HD), F32),
            pltpu.VMEM((PARTS, ROWS, PART), BF16),
            pltpu.VMEM((2, PARTS, 8 * CAP, PART), BF16),
            pltpu.VMEM((PARTS, 2 * CAP, PART), BF16),
            pltpu.VMEM((2, 2, TOK, 8 * CAP), BF16),
            pltpu.VMEM((2, TOK, 2 * CAP), BF16),
            pltpu.VMEM((2, PARTS, TOK, PART), BF16),
            pltpu.VMEM((2, PARTS, TOK, PART), BF16),
            dma((3, 20)),
            dma((3, 20)),
            dma((2, 2, 2, 2)),
            dma((2, 2, 2)),
            dma((2, 2)),
            dma((2, 5, 2)),
            dma((MEMS, 2)),
            dma((2,)),
            dma((4,)),
            dma((2,)),
            dma((4, PARTS, 2, 2)),
            dma((12, PARTS)),
            dma((2, 7, PARTS)),
            dma((PARTS, 2)),
            dma((2, PARTS, 2)),
        ],
        compiler_params=pltpu.CompilerParams(
            collective_id=0, has_side_effects=True, vmem_limit_bytes=58 * 2**20
        ),
        name="memories",
    )(hidden, routes.T, gate_levels.T, query_weight, key_weight, value_weight)


def solution(mesh):
    return jax.shard_map(
        on_device,
        mesh=mesh,
        in_specs=(
            P(("seq", "mem"), None),
            P(("seq", "mem"), None),
            P(("seq", "mem"), None),
            P("seq", None),
            P("mem", "seq", None),
            P("mem", "seq", None),
        ),
        out_specs=P(("seq", "mem"), None),
        check_vma=False,
    )
```

```python
import jax
import jax.numpy as jnp
from jax import lax
from jax.experimental import pallas as pl
from jax.experimental.pallas import tpu as pltpu
from jax.sharding import PartitionSpec as P

D = 2048
HD = 1024
HEADS = 8
DK = 128
TOK = 256
CAP = 64
MEMS = 16
SIDE = 4
RING = 8
ROWS = MEMS * CAP
HALF = HD // 2
PARTS = 4
PART = HD // PARTS
BLOCK = 256
BF16 = jnp.bfloat16
F32 = jnp.float32
MESH = pl.DeviceIdType.MESH


def tiles(total, width, body):
    @pl.loop(0, total // width)
    def _(step):
        body(pl.ds(pl.multiple_of(step * width, width), width))


def weight_stream(whole, own, base, n, x_first, y, x, send_sems, recv_sems):
    f = x_first * x + (1 - x_first) * y
    g = x_first * y + (1 - x_first) * x

    def place(i, j):
        a, b = lax.rem(f + i + SIDE, SIDE), lax.rem(g + j + SIDE, SIDE)
        return x_first * (b * SIDE + a) + (1 - x_first) * (a * SIDE + b)

    def piece(i, j, part=None):
        start, rows = base, n
        if part is not None:
            start, rows = base + part * (n // 2), n // 2
        return whole.at[place(i, j), pl.ds(start, rows), :]

    def send(number, src, dst, i, j):
        return pltpu.make_async_remote_copy(
            src_ref=src,
            dst_ref=dst,
            send_sem=send_sems.at[number],
            recv_sem=recv_sems.at[number],
            device_id={"seq": place(i, j)},
            device_id_type=MESH,
        )

    def relay(number, i, j, part, di, dj):
        return send(number, piece(i, j, part), piece(i, j, part), di, dj)

    first = [send(c, own, piece(0, 0), *to) for c, to in enumerate(((1, 0), (-1, 0), (0, 1), (0, -1)))]
    copies = first + [
        relay(4, -1, 0, 0, 1, 0),
        relay(5, 1, 0, 1, -1, 0),
        relay(6, 0, -1, 0, 0, 1),
        relay(7, 0, 1, 1, 0, -1),
        relay(8, -1, 0, None, 0, 1),
        relay(9, -1, 0, None, 0, -1),
        relay(10, 1, 0, None, 0, 1),
        relay(11, 1, 0, None, 0, -1),
        relay(12, 2, 0, None, 0, 1),
        relay(13, 2, 0, None, 0, -1),
        relay(14, -1, -1, 0, 0, 1),
        relay(15, -1, 1, 1, 0, -1),
        relay(16, 1, -1, 0, 0, 1),
        relay(17, 1, 1, 1, 0, -1),
        relay(18, 2, -1, 0, 0, 1),
        relay(19, 2, 1, 1, 0, -1),
    ]
    return copies


def kernel(
    hid, routes, levels, qw, kw, vw, out,
    raw, tab, rows_in, near_stage, stage, sib_stage, wq, wk, wv, q, k, v, xs,
    block_states, total, entering, before, s_send, s_recv, reads, normed,
    ret, own_ret, gates, own_gates, part_out, part_in,
    w_send, w_recv, raw_sems, tab_sems, near_send, set_send, set_recv, sib_send, local_sems, swap_sems,
    state_sems, ret_send, ret_recv, own_ret_sems, part_sems,
):
    me, group = lax.axis_index("mem"), lax.axis_index("seq")
    z, core = me // 2, me % 2
    y, x = group // SIDE, group % SIDE

    def mem(chip, c):
        return lax.rem(chip + RING, RING) * 2 + c

    def rcopy(src, dst, send_sem, recv_sem, device):
        return pltpu.make_async_remote_copy(
            src_ref=src, dst_ref=dst, send_sem=send_sem, recv_sem=recv_sem, device_id=device, device_id_type=MESH
        )

    def spot(source):
        return pl.ds(pl.multiple_of(source * CAP, CAP), CAP)

    def columns(part):
        return pl.ds(part * HD, HD)

    sent = []

    def go(copy):
        copy.start()
        sent.append(copy)
        return copy

    other = mem(z, 1 - core)
    barrier = pltpu.get_barrier_semaphore()
    peers = [{"mem": other}]
    peers += [{"mem": mem(z - 1, core)}, {"mem": mem(z + 1, core)}]
    for dx, dy in ((1, 0), (3, 0), (0, 1), (0, 3)):
        peers.append({"seq": lax.rem(y + dy, SIDE) * SIDE + lax.rem(x + dx, SIDE)})
    for peer in peers:
        pl.semaphore_signal(barrier, inc=1, device_id=peer, device_id_type=MESH)

    mine = [
        pltpu.make_async_copy(hid, raw.at[2], local_sems.at[0]),
        pltpu.make_async_copy(kw.at[0], wk.at[group], local_sems.at[1]),
        pltpu.make_async_copy(vw.at[0], wv.at[group], local_sems.at[2]),
    ]
    half = pl.multiple_of(core * CAP, CAP)
    mine.append(
        pltpu.make_async_copy(qw.at[pl.ds(half, CAP), :], wq.at[group, pl.ds(half, CAP), :], local_sems.at[3])
    )
    for copy in mine:
        copy.start()
    ids = lax.broadcasted_iota(jnp.int32, (MEMS, TOK), 0)
    hit0, hit1 = routes[0:1, :] == ids, routes[1:2, :] == ids
    earlier = lax.broadcasted_iota(jnp.int32, (TOK, TOK), 0) < lax.broadcasted_iota(jnp.int32, (TOK, TOK), 1)
    hits = jnp.where(hit0 | hit1, 1.0, 0.0)
    place = jnp.dot(hits.astype(BF16), jnp.where(earlier, 1.0, 0.0).astype(BF16), preferred_element_type=F32)
    lev0, lev1 = levels[0:1, :].astype(F32), levels[1:2, :].astype(F32)
    both = lev0 + lev1
    tab[2, 0:MEMS, :] = jnp.where(hits > 0, place, -1.0)
    tab[2, MEMS : 2 * MEMS, :] = jnp.where(hit0, lev0 / both, 0.0) + jnp.where(hit1, lev1 / both, 0.0)

    pl.semaphore_wait(barrier, len(peers))

    raws, tabs = [], []

    def pass_tables(hop):
        for side, step in ((0, 1), (1, -1)):
            src = tab.at[2] if hop == 0 else tab.at[side]
            sems, to = tab_sems.at[hop, side], {"mem": mem(z + step, core)}
            tabs.append(go(rcopy(src, tab.at[side + 3 * hop], sems.at[0], sems.at[1], to)))

    def pass_rows(hop, part):
        for side, step in ((0, 1), (1, -1)):
            cols, sems = columns(part), raw_sems.at[hop, side, part]
            src = hid.at[:, cols] if hop == 0 else raw.at[side, :, cols]
            to = {"mem": mem(z + step, core)}
            raws.append(go(rcopy(src, raw.at[side + 3 * hop, :, cols], sems.at[0], sems.at[1], to)))

    pass_tables(0)
    pass_rows(0, 0)
    pass_rows(0, 1)
    own_q = qw.at[pl.ds(half, CAP), :]
    keyed = [
        weight_stream(wk, kw.at[0], 0, 128, 1, y, x, w_send.at[0], w_recv.at[0]),
        weight_stream(wv, vw.at[0], 0, 128, 0, y, x, w_send.at[1], w_recv.at[1]),
    ]
    asked = [weight_stream(wq, own_q, half, CAP, 1 - core, y, x, w_send.at[2], w_recv.at[2])]

    def start(streams, *numbers):
        for number in numbers:
            for copies in streams:
                go(copies[number])

    def arrive(streams, *numbers):
        for number in numbers:
            for copies in streams:
                copies[number].wait_recv()

    start(keyed, 0, 1, 2, 3)

    slot = lax.broadcasted_iota(jnp.int32, (CAP, TOK), 0).astype(F32)

    def matches(index, mems):
        return [slot == tab[index, pl.ds(e, 1), :] for e in mems]

    def chosen(index, mems):
        ones = [jnp.where(m, 1.0, 0.0).astype(BF16) for m in matches(index, mems)]
        return jnp.concatenate(ones, axis=0)

    def pack(index, ones, dest, part):
        def body(cols):
            cols = pl.ds(part * HD + cols.start, cols.size)
            dest[:, cols] = jnp.dot(ones, raw[index, :, cols], preferred_element_type=F32).astype(BF16)

        tiles(HD, 512, body)

    def mixing(index, mems, dest, width):
        parts = [
            jnp.where(m, tab[index, pl.ds(MEMS + e, 1), :], 0.0) for m, e in zip(matches(index, mems), mems)
        ]
        if width > len(mems) * CAP:
            parts.append(jnp.zeros((width - len(mems) * CAP, TOK), F32))
        weights = jnp.concatenate(parts, axis=0).T
        high = weights.astype(BF16)
        dest[0] = high
        dest[1] = (weights - high.astype(F32)).astype(BF16)

    def served(side):
        step = 1 - 2 * side
        return [
            me, other,
            mem(z + step, 0), mem(z + step, 1),
            mem(z + 2 * step, 0), mem(z + 2 * step, 1),
            mem(z + 3 * step, side),
        ]

    for copy in mine:
        copy.wait()
    for part in (0, 1):
        pack(2, chosen(2, [me, other]), sib_stage, part)
    for part in (0, 1):
        cols = columns(part)
        src, dst = sib_stage.at[pl.ds(CAP, CAP), cols], rows_in.at[spot(me), cols]
        go(rcopy(src, dst, sib_send.at[part], set_recv.at[me, part], {"mem": other}))
    rows_in[spot(me), :] = sib_stage[0:CAP, :]
    mixing(2, [me, other], own_gates, 2 * CAP)

    arrive(keyed, 0, 1, 2, 3)
    start(keyed, 8, 9, 10, 11, 4, 5, 6, 7)
    start(asked, 0, 1, 2, 3)

    for side in (0, 1):
        tabs[side].wait_recv()
    pass_tables(1)
    for part in (0, 1):
        cols = columns(part)
        for side in (0, 1):
            raws[2 * part + side].wait_recv()
        pass_rows(1, part)
        for side in (0, 1):
            origin = mem(z - 1 + 2 * side, core)
            pack(side, chosen(side, [me, other]), near_stage.at[side], part)
            src, dst = near_stage.at[side, pl.ds(CAP, CAP), cols], rows_in.at[spot(origin), cols]
            go(rcopy(src, dst, near_send.at[side, part], set_recv.at[origin, part], {"mem": other}))
            rows_in[spot(origin), cols] = near_stage[side, 0:CAP, cols]

    def await_rows(sources):
        for source in sources:
            for part in (0, 1):
                there = rows_in.at[spot(source), columns(part)]
                rcopy(there, there, sib_send.at[part], set_recv.at[source, part], {"mem": other}).wait_recv()

    arrive(keyed, 4, 5, 8, 9, 10, 11)
    start(keyed, 12, 13, 14, 15, 16, 17)
    arrive(asked, 0, 1, 2, 3)
    start(asked, 8, 9, 10, 11, 4, 5, 6, 7)
    await_rows([other, mem(z - 1, 1 - core), mem(z + 1, 1 - core)])

    def further(side):
        step = 1 - 2 * side
        return [me, other, mem(z + step, 0), mem(z + step, 1), mem(z + 2 * step, side)]

    for side in (0, 1):
        tabs[2 + side].wait_recv()
    far_ones = [chosen(3 + side, further(side)) for side in (0, 1)]
    for part in (0, 1):
        for side in (0, 1):
            origin = mem(z - 2 + 4 * side, core)
            mems = further(side)
            cols = columns(part)
            raws[4 + 2 * part + side].wait_recv()
            pack(3 + side, far_ones[side], stage.at[side], part)
            for number in (2, 3, 4, 1):
                src, dst = stage.at[side, pl.ds(number * CAP, CAP), cols], rows_in.at[spot(origin), cols]
                sems = (set_send.at[side, number, part], set_recv.at[origin, part])
                go(rcopy(src, dst, *sems, {"mem": mems[number]}))
            rows_in[spot(origin), cols] = stage[side, 0:CAP, cols]
        if part == 0:
            arrive(keyed, 12, 13)
            start(keyed, 18, 19)
            arrive(asked, 4, 5, 8, 9, 10, 11)
            start(asked, 12, 13, 14, 15, 16, 17)

    for side in (0, 1):
        mixing(side, served(side), gates.at[side], 8 * CAP)
        ret[side, :, 7 * CAP : 8 * CAP, :] = jnp.zeros((PARTS, CAP, PART), BF16)
    arrive(keyed, 6, 7, 14, 15, 16, 17, 18, 19)

    def take(first, sources):
        for n, source in enumerate(sources):
            xs[first + n * CAP : first + (n + 1) * CAP, :] = rows_in[spot(source), :]

    def project(first, sources, weight, dest):
        many = len(sources) * CAP
        width = HD if many <= 384 else HALF

        def body(cols):
            w = weight[:, :, cols].reshape(D, width)
            result = jnp.dot(xs[first : first + many, :], w, preferred_element_type=F32).astype(BF16)
            for n, source in enumerate(sources):
                dest[spot(source), cols] = result[n * CAP : (n + 1) * CAP]

        tiles(HD, width, body)

    causal = lax.broadcasted_iota(jnp.int32, (BLOCK, BLOCK), 0) >= lax.broadcasted_iota(
        jnp.int32, (BLOCK, BLOCK), 1
    )
    first_block = lax.rem((z + 1) // 2 + 3, 4)
    turn = [lax.rem(first_block + n, 4) for n in range(4)]

    def head_cols(h):
        return pl.ds(pl.multiple_of(h * DK, DK), DK)

    def state_rows(h):
        return pl.ds(pl.multiple_of((lax.rem(h, 2) * (HEADS // 2) + h // 2) * DK, DK), DK)

    def attend(blocks, h):
        cols = head_cols(h)
        for b in blocks:
            rows = pl.ds(pl.multiple_of(b * BLOCK, BLOCK), BLOCK)
            scores = lax.dot_general(
                q[rows, cols], k[rows, cols], (((1,), (1,)), ((), ())), preferred_element_type=F32
            )
            scores = jnp.where(causal, scores, 0.0).astype(BF16)
            reads[rows, cols] = jnp.dot(scores, v[rows, cols], preferred_element_type=F32)

    def add_up(blocks, h):
        cols = head_cols(h)
        for b in blocks:
            rows = pl.ds(pl.multiple_of(b * BLOCK, BLOCK), BLOCK)
            block_states[b, state_rows(h), :] = lax.dot_general(
                k[rows, cols], v[rows, cols], (((0,), (0,)), ((), ())), preferred_element_type=F32
            )

    near = [me, other] + [mem(z + d, c) for d in (-1, 1) for c in (core, 1 - core)]
    take(0, near)
    project(0, near, wk, k)
    arrive(asked, 12, 13)
    start(asked, 18, 19)
    project(0, near, wv, v)
    arrive(asked, 6, 7, 14, 15, 16, 17, 18, 19)
    halves = wq.at[:, pl.ds(half, CAP), :]
    swap = go(rcopy(halves, halves, swap_sems.at[0], swap_sems.at[1], {"mem": other}))
    middle = [mem(z + d, c) for d in (-2, 2) for c in (0, 1)]
    await_rows([mem(z + d, 1 - core) for d in (-2, 2)])
    take(384, middle)
    project(384, middle, wk, k)
    project(384, middle, wv, v)

    @pl.loop(0, HEADS)
    def _(h):
        add_up(turn[:2], h)

    far = [mem(z + d, c) for d in (-3, 3) for c in (0, 1)]
    swap.wait_recv()
    project(0, near + middle, wq, q)

    @pl.loop(0, 2)
    def _(h):
        attend(turn[:2], h)

    await_rows(far)
    take(640, far)
    project(640, far, wk, k)
    project(640, far, wv, v)
    last_ones = [mem(z + 4, c) for c in (0, 1)]
    await_rows(last_ones)
    take(896, last_ones)
    project(896, last_ones, wk, k)
    project(896, last_ones, wv, v)

    def at(row, column):
        return row * SIDE + column

    y1, y3 = y + 1 - 2 * (y % 2), SIDE - 1 - y
    x1, x3 = x + 1 - 2 * (x % 2), SIDE - 1 - x
    sums = [(at(y, x1), x % 2), (at(y, x3), x // 2), (at(y1, x), y % 2), (at(y3, x), y // 2)]
    befores = [(at(y3, x), 1 - y // 2), (at(y1, x), 1 - y % 2), (at(y, x3), 1 - x // 2), (at(y, x1), 1 - x % 2)]
    entering[...] = jnp.zeros_like(entering)
    moving = {}

    def low_high(pair):
        return pl.ds(pair * DK, DK), pl.ds(HALF + pair * DK, DK)

    def push(step, pair):
        low, high = low_high(pair)
        s_send[step, low, :] = total[low, :].astype(BF16)
        s_send[step, high, :] = (entering[high, :] + total[high, :] * befores[step][1].astype(F32)).astype(BF16)
        for stream, (rows, to) in enumerate(((low, sums[step][0]), (high, befores[step][0]))):
            sems = state_sems.at[step, pair, stream]
            src, dst = s_send.at[step, rows], s_recv.at[step, rows]
            moving[step, pair, stream] = go(rcopy(src, dst, sems.at[0], sems.at[1], {"seq": to}))

    def pull(step, pair):
        low, high = low_high(pair)
        moving[step, pair, 0].wait_recv()
        moving[step, pair, 1].wait_recv()
        theirs = s_recv[step, low, :].astype(F32)
        entering[low, :] += theirs * sums[step][1].astype(F32)
        if step < 3:
            total[low, :] += theirs
        entering[high, :] += s_recv[step, high, :].astype(F32)

    for pair in range(PARTS):
        for h in (2 * pair, 2 * pair + 1):
            add_up(turn[2:], h)
        for rows in low_high(pair):
            total[rows, :] = (block_states[0, rows, :] + block_states[1, rows, :]) + (
                block_states[2, rows, :] + block_states[3, rows, :]
            )
        push(0, pair)
    project(640, far + last_ones, wq, q)
    running = jnp.zeros((HD, DK), F32)
    for b in range(4):
        before[b] = running.astype(BF16)
        running = running + block_states[b]
    tasks = [(turn[2:], h) for h in range(HEADS)] + [(turn[:2], h) for h in range(2, HEADS)]
    for step in range(3):
        for pair in range(PARTS):
            for task in tasks[step * PARTS + pair :: 3 * PARTS]:
                attend(*task)
            pull(step, pair)
            push(step + 1, pair)

    def finish(chip, part):
        chip = lax.rem(chip + RING, RING)
        rows = pl.ds(pl.multiple_of(chip * 128, 128), 128)
        for h in (2 * part, 2 * part + 1):
            cols = slice(h * DK, (h + 1) * DK)
            place = h % 2 * (HEADS // 2) + h // 2
            states = slice(place * DK, (place + 1) * DK)
            state = (entering[states, :] + before[chip // 2, states, :].astype(F32)).astype(BF16)
            read = reads[rows, cols] + jnp.dot(q[rows, cols], state, preferred_element_type=F32)
            scale = lax.rsqrt(jnp.mean(read * read, axis=1, keepdims=True) + 1e-6)
            normed[part, rows, h % 2 * DK : (h % 2 + 1) * DK] = (read * scale).astype(BF16)

    def give(part, source, node, side, number, sem):
        src, dst = normed.at[part, spot(source)], ret.at[side, part, spot(number)]
        go(rcopy(src, dst, ret_send.at[sem, part], ret_recv.at[side, number, part], {"mem": node}))

    back = []
    for part in range(PARTS):
        pull(3, part)
        finish(z + 4, part)
        for c in (0, 1):
            give(part, mem(z + 4, c), mem(z + 5 - 2 * core, c), core, 6, c)
        sem = 2
        for distance in (3, 2):
            for side in (0, 1):
                step = 1 - 2 * side
                finish(z - distance * step, part)
                for c in (0, 1):
                    source, node = mem(z - distance * step, c), mem(z - (distance - 1) * step, c)
                    give(part, source, node, side, 2 * (distance - 1) + core, sem)
                    sem += 1
        for side in (0, 1):
            chip = z - 1 + 2 * side
            finish(chip, part)
            give(part, mem(chip, 1 - core), other, side, 1, sem)
            sem += 1
            ret[side, part, 0:CAP, :] = normed[part, spot(mem(chip, core)), :]
        finish(z, part)
        src, dst = normed.at[part, spot(other)], own_ret.at[part, pl.ds(CAP, CAP), :]
        back.append(go(rcopy(src, dst, own_ret_sems.at[part, 0], own_ret_sems.at[part, 1], {"mem": other})))
        own_ret[part, 0:CAP, :] = normed[part, spot(me), :]

    parts = []
    for part in range(PARTS):
        for side in (0, 1):
            for number in range(1, 7):
                there = ret.at[side, part, pl.ds(number * CAP, CAP), :]
                sems = (ret_send.at[0, 0], ret_recv.at[side, number, part])
                rcopy(there, there, *sems, {"mem": other}).wait_recv()
            rows = ret[side, part]
            result = jnp.dot(gates[side, 0], rows, preferred_element_type=F32)
            result = result + jnp.dot(gates[side, 1], rows, preferred_element_type=F32)
            part_out[side, part] = result.astype(BF16)
            to = {"mem": mem(z - 1 + 2 * side, core)}
            src, dst, sems = part_out.at[side, part], part_in.at[side, part], part_sems.at[side, part]
            parts.append(go(rcopy(src, dst, sems.at[0], sems.at[1], to)))
    for part in range(PARTS):
        back[part].wait_recv()
        rows = own_ret[part]
        result = jnp.dot(own_gates[0], rows, preferred_element_type=F32)
        result = result + jnp.dot(own_gates[1], rows, preferred_element_type=F32)
        for side in (0, 1):
            parts[2 * part + side].wait_recv()
        result = result + part_in[0, part].astype(F32) + part_in[1, part].astype(F32)
        out[:, part * PART : (part + 1) * PART] = result.astype(BF16)
    for copy in sent:
        copy.wait_send()


def on_device(hidden, routes, gate_levels, query_weight, key_weight, value_weight):
    dma = pltpu.SemaphoreType.DMA
    whole = pl.BlockSpec(memory_space=pl.ANY)
    near = pl.BlockSpec(memory_space=pltpu.VMEM)
    return pl.pallas_call(
        kernel,
        out_shape=jax.ShapeDtypeStruct((TOK, HD), BF16),
        in_specs=[whole, near, near, whole, whole, whole],
        out_specs=near,
        scratch_shapes=[
            pltpu.VMEM((5, TOK, D), BF16),
            pltpu.VMEM((5, 2 * MEMS, TOK), F32),
            pltpu.VMEM((ROWS, D), BF16),
            pltpu.VMEM((2, 2 * CAP, D), BF16),
            pltpu.VMEM((2, 5 * CAP, D), BF16),
            pltpu.VMEM((2 * CAP, D), BF16),
            pltpu.VMEM((16, 128, HD), BF16),
            pltpu.VMEM((16, 128, HD), BF16),
            pltpu.VMEM((16, 128, HD), BF16),
            pltpu.VMEM((ROWS, HD), BF16),
            pltpu.VMEM((ROWS, HD), BF16),
            pltpu.VMEM((ROWS, HD), BF16),
            pltpu.VMEM((ROWS, D), BF16),
            pltpu.VMEM((4, HD, DK), F32),
            pltpu.VMEM((HD, DK), F32),
            pltpu.VMEM((HD, DK), F32),
            pltpu.VMEM((4, HD, DK), BF16),
            pltpu.VMEM((4, HD, DK), BF16),
            pltpu.VMEM((4, HD, DK), BF16),
            pltpu.VMEM((ROWS, HD), F32),
            pltpu.VMEM((PARTS, ROWS, PART), BF16),
            pltpu.VMEM((2, PARTS, 8 * CAP, PART), BF16),
            pltpu.VMEM((PARTS, 2 * CAP, PART), BF16),
            pltpu.VMEM((2, 2, TOK, 8 * CAP), BF16),
            pltpu.VMEM((2, TOK, 2 * CAP), BF16),
            pltpu.VMEM((2, PARTS, TOK, PART), BF16),
            pltpu.VMEM((2, PARTS, TOK, PART), BF16),
            dma((3, 20)),
            dma((3, 20)),
            dma((2, 2, 2, 2)),
            dma((2, 2, 2)),
            dma((2, 2)),
            dma((2, 5, 2)),
            dma((MEMS, 2)),
            dma((2,)),
            dma((4,)),
            dma((2,)),
            dma((4, PARTS, 2, 2)),
            dma((12, PARTS)),
            dma((2, 7, PARTS)),
            dma((PARTS, 2)),
            dma((2, PARTS, 2)),
        ],
        compiler_params=pltpu.CompilerParams(
            collective_id=0, has_side_effects=True, vmem_limit_bytes=58 * 2**20
        ),
        name="memories",
    )(hidden, routes.T, gate_levels.T, query_weight, key_weight, value_weight)


def solution(mesh):
    return jax.shard_map(
        on_device,
        mesh=mesh,
        in_specs=(
            P(("seq", "mem"), None),
            P(("seq", "mem"), None),
            P(("seq", "mem"), None),
            P("seq", None),
            P("mem", "seq", None),
            P("mem", "seq", None),
        ),
        out_specs=P(("seq", "mem"), None),
        check_vma=False,
    )
```

```python
import jax
import jax.numpy as jnp
from jax import lax
from jax.experimental import pallas as pl
from jax.experimental.pallas import tpu as pltpu
from jax.sharding import PartitionSpec as P

D = 2048
HD = 1024
HEADS = 8
DK = 128
TOK = 256
CAP = 64
MEMS = 16
SIDE = 4
RING = 8
ROWS = MEMS * CAP
HALF = HD // 2
PARTS = 4
PART = HD // PARTS
BLOCK = 256
BF16 = jnp.bfloat16
F32 = jnp.float32
MESH = pl.DeviceIdType.MESH


def tiles(total, width, body):
    @pl.loop(0, total // width)
    def _(step):
        body(pl.ds(pl.multiple_of(step * width, width), width))


def weight_stream(whole, own, base, n, x_first, y, x, send_sems, recv_sems):
    f = x_first * x + (1 - x_first) * y
    g = x_first * y + (1 - x_first) * x

    def place(i, j):
        a, b = lax.rem(f + i + SIDE, SIDE), lax.rem(g + j + SIDE, SIDE)
        return x_first * (b * SIDE + a) + (1 - x_first) * (a * SIDE + b)

    def piece(i, j, part=None):
        start, rows = base, n
        if part is not None:
            start, rows = base + part * (n // 2), n // 2
        return whole.at[place(i, j), pl.ds(start, rows), :]

    def send(number, src, dst, i, j):
        return pltpu.make_async_remote_copy(
            src_ref=src,
            dst_ref=dst,
            send_sem=send_sems.at[number],
            recv_sem=recv_sems.at[number],
            device_id={"seq": place(i, j)},
            device_id_type=MESH,
        )

    def relay(number, i, j, part, di, dj):
        return send(number, piece(i, j, part), piece(i, j, part), di, dj)

    first = [send(c, own, piece(0, 0), *to) for c, to in enumerate(((1, 0), (-1, 0), (0, 1), (0, -1)))]
    copies = first + [
        relay(4, -1, 0, 0, 1, 0),
        relay(5, 1, 0, 1, -1, 0),
        relay(6, 0, -1, 0, 0, 1),
        relay(7, 0, 1, 1, 0, -1),
        relay(8, -1, 0, None, 0, 1),
        relay(9, -1, 0, None, 0, -1),
        relay(10, 1, 0, None, 0, 1),
        relay(11, 1, 0, None, 0, -1),
        relay(12, 2, 0, None, 0, 1),
        relay(13, 2, 0, None, 0, -1),
        relay(14, -1, -1, 0, 0, 1),
        relay(15, -1, 1, 1, 0, -1),
        relay(16, 1, -1, 0, 0, 1),
        relay(17, 1, 1, 1, 0, -1),
        relay(18, 2, -1, 0, 0, 1),
        relay(19, 2, 1, 1, 0, -1),
    ]
    return copies


def kernel(
    hid, routes, levels, qw, kw, vw, out,
    raw, tab, rows_in, near_stage, stage, sib_stage, wq, wk, wv, q, k, v, xs,
    block_states, total, entering, before, s_send, s_recv, reads, normed,
    ret, own_ret, gates, own_gates, part_out, part_in,
    w_send, w_recv, raw_sems, tab_sems, near_send, set_send, set_recv, sib_send, local_sems, swap_sems,
    state_sems, ret_send, ret_recv, own_ret_sems, part_sems,
):
    me, group = lax.axis_index("mem"), lax.axis_index("seq")
    z, core = me // 2, me % 2
    y, x = group // SIDE, group % SIDE

    def mem(chip, c):
        return lax.rem(chip + RING, RING) * 2 + c

    def rcopy(src, dst, send_sem, recv_sem, device):
        return pltpu.make_async_remote_copy(
            src_ref=src, dst_ref=dst, send_sem=send_sem, recv_sem=recv_sem, device_id=device, device_id_type=MESH
        )

    def spot(source):
        return pl.ds(pl.multiple_of(source * CAP, CAP), CAP)

    def columns(part):
        return pl.ds(part * HD, HD)

    sent = []

    def go(copy):
        copy.start()
        sent.append(copy)
        return copy

    other = mem(z, 1 - core)
    barrier = pltpu.get_barrier_semaphore()
    peers = [{"mem": other}]
    peers += [{"mem": mem(z - 1, core)}, {"mem": mem(z + 1, core)}]
    for dx, dy in ((1, 0), (3, 0), (0, 1), (0, 3)):
        peers.append({"seq": lax.rem(y + dy, SIDE) * SIDE + lax.rem(x + dx, SIDE)})
    for peer in peers:
        pl.semaphore_signal(barrier, inc=1, device_id=peer, device_id_type=MESH)

    mine = [
        pltpu.make_async_copy(hid, raw.at[2], local_sems.at[0]),
        pltpu.make_async_copy(kw.at[0], wk.at[group], local_sems.at[1]),
        pltpu.make_async_copy(vw.at[0], wv.at[group], local_sems.at[2]),
    ]
    half = pl.multiple_of(core * CAP, CAP)
    mine.append(
        pltpu.make_async_copy(qw.at[pl.ds(half, CAP), :], wq.at[group, pl.ds(half, CAP), :], local_sems.at[3])
    )
    for copy in mine:
        copy.start()
    ids = lax.broadcasted_iota(jnp.int32, (MEMS, TOK), 0)
    hit0, hit1 = routes[0:1, :] == ids, routes[1:2, :] == ids
    earlier = lax.broadcasted_iota(jnp.int32, (TOK, TOK), 0) < lax.broadcasted_iota(jnp.int32, (TOK, TOK), 1)
    hits = jnp.where(hit0 | hit1, 1.0, 0.0)
    place = jnp.dot(hits.astype(BF16), jnp.where(earlier, 1.0, 0.0).astype(BF16), preferred_element_type=F32)
    lev0, lev1 = levels[0:1, :].astype(F32), levels[1:2, :].astype(F32)
    both = lev0 + lev1
    tab[2, 0:MEMS, :] = jnp.where(hits > 0, place, -1.0)
    tab[2, MEMS : 2 * MEMS, :] = jnp.where(hit0, lev0 / both, 0.0) + jnp.where(hit1, lev1 / both, 0.0)

    pl.semaphore_wait(barrier, len(peers))

    raws, tabs = [], []

    def pass_tables(hop):
        for side, step in ((0, 1), (1, -1)):
            src = tab.at[2] if hop == 0 else tab.at[side]
            sems, to = tab_sems.at[hop, side], {"mem": mem(z + step, core)}
            tabs.append(go(rcopy(src, tab.at[side + 3 * hop], sems.at[0], sems.at[1], to)))

    def pass_rows(hop, part):
        for side, step in ((0, 1), (1, -1)):
            cols, sems = columns(part), raw_sems.at[hop, side, part]
            src = hid.at[:, cols] if hop == 0 else raw.at[side, :, cols]
            to = {"mem": mem(z + step, core)}
            raws.append(go(rcopy(src, raw.at[side + 3 * hop, :, cols], sems.at[0], sems.at[1], to)))

    pass_tables(0)
    pass_rows(0, 0)
    pass_rows(0, 1)
    own_q = qw.at[pl.ds(half, CAP), :]
    keyed = [
        weight_stream(wk, kw.at[0], 0, 128, 1, y, x, w_send.at[0], w_recv.at[0]),
        weight_stream(wv, vw.at[0], 0, 128, 0, y, x, w_send.at[1], w_recv.at[1]),
    ]
    asked = [weight_stream(wq, own_q, half, CAP, 1 - core, y, x, w_send.at[2], w_recv.at[2])]

    def start(streams, *numbers):
        for number in numbers:
            for copies in streams:
                go(copies[number])

    def arrive(streams, *numbers):
        for number in numbers:
            for copies in streams:
                copies[number].wait_recv()

    start(keyed, 0, 1, 2, 3)

    slot = lax.broadcasted_iota(jnp.int32, (CAP, TOK), 0).astype(F32)

    def matches(index, mems):
        return [slot == tab[index, pl.ds(e, 1), :] for e in mems]

    def chosen(index, mems):
        ones = [jnp.where(m, 1.0, 0.0).astype(BF16) for m in matches(index, mems)]
        return jnp.concatenate(ones, axis=0)

    def pack(index, ones, dest, part):
        def body(cols):
            cols = pl.ds(part * HD + cols.start, cols.size)
            dest[:, cols] = jnp.dot(ones, raw[index, :, cols], preferred_element_type=F32).astype(BF16)

        tiles(HD, 512, body)

    def mixing(index, mems, dest, width):
        parts = [
            jnp.where(m, tab[index, pl.ds(MEMS + e, 1), :], 0.0) for m, e in zip(matches(index, mems), mems)
        ]
        if width > len(mems) * CAP:
            parts.append(jnp.zeros((width - len(mems) * CAP, TOK), F32))
        weights = jnp.concatenate(parts, axis=0).T
        high = weights.astype(BF16)
        dest[0] = high
        dest[1] = (weights - high.astype(F32)).astype(BF16)

    def served(side):
        step = 1 - 2 * side
        return [
            me, other,
            mem(z + step, 0), mem(z + step, 1),
            mem(z + 2 * step, 0), mem(z + 2 * step, 1),
            mem(z + 3 * step, side),
        ]

    for copy in mine:
        copy.wait()
    for part in (0, 1):
        pack(2, chosen(2, [me, other]), sib_stage, part)
    for part in (0, 1):
        cols = columns(part)
        src, dst = sib_stage.at[pl.ds(CAP, CAP), cols], rows_in.at[spot(me), cols]
        go(rcopy(src, dst, sib_send.at[part], set_recv.at[me, part], {"mem": other}))
    rows_in[spot(me), :] = sib_stage[0:CAP, :]
    mixing(2, [me, other], own_gates, 2 * CAP)

    arrive(keyed, 0, 1, 2, 3)
    start(keyed, 8, 9, 10, 11, 4, 5, 6, 7)
    start(asked, 0, 1, 2, 3)

    for side in (0, 1):
        tabs[side].wait_recv()
    pass_tables(1)
    for part in (0, 1):
        cols = columns(part)
        for side in (0, 1):
            raws[2 * part + side].wait_recv()
        pass_rows(1, part)
        for side in (0, 1):
            origin = mem(z - 1 + 2 * side, core)
            pack(side, chosen(side, [me, other]), near_stage.at[side], part)
            src, dst = near_stage.at[side, pl.ds(CAP, CAP), cols], rows_in.at[spot(origin), cols]
            go(rcopy(src, dst, near_send.at[side, part], set_recv.at[origin, part], {"mem": other}))
            rows_in[spot(origin), cols] = near_stage[side, 0:CAP, cols]

    def await_rows(sources):
        for source in sources:
            for part in (0, 1):
                there = rows_in.at[spot(source), columns(part)]
                rcopy(there, there, sib_send.at[part], set_recv.at[source, part], {"mem": other}).wait_recv()

    arrive(keyed, 4, 5, 8, 9, 10, 11)
    start(keyed, 12, 13, 14, 15, 16, 17)
    arrive(asked, 0, 1, 2, 3)
    start(asked, 8, 9, 10, 11, 4, 5, 6, 7)
    await_rows([other, mem(z - 1, 1 - core), mem(z + 1, 1 - core)])

    def further(side):
        step = 1 - 2 * side
        return [me, other, mem(z + step, 0), mem(z + step, 1), mem(z + 2 * step, side)]

    for side in (0, 1):
        tabs[2 + side].wait_recv()
    far_ones = [chosen(3 + side, further(side)) for side in (0, 1)]
    for part in (0, 1):
        for side in (0, 1):
            origin = mem(z - 2 + 4 * side, core)
            mems = further(side)
            cols = columns(part)
            raws[4 + 2 * part + side].wait_recv()
            pack(3 + side, far_ones[side], stage.at[side], part)
            for number in (2, 3, 4, 1):
                src, dst = stage.at[side, pl.ds(number * CAP, CAP), cols], rows_in.at[spot(origin), cols]
                sems = (set_send.at[side, number, part], set_recv.at[origin, part])
                go(rcopy(src, dst, *sems, {"mem": mems[number]}))
            rows_in[spot(origin), cols] = stage[side, 0:CAP, cols]
        if part == 0:
            arrive(keyed, 12, 13)
            start(keyed, 18, 19)
            arrive(asked, 4, 5, 8, 9, 10, 11)
            start(asked, 12, 13, 14, 15, 16, 17)

    for side in (0, 1):
        mixing(side, served(side), gates.at[side], 8 * CAP)
        ret[side, :, 7 * CAP : 8 * CAP, :] = jnp.zeros((PARTS, CAP, PART), BF16)
    arrive(keyed, 6, 7, 14, 15, 16, 17, 18, 19)

    def take(first, sources):
        for n, source in enumerate(sources):
            xs[first + n * CAP : first + (n + 1) * CAP, :] = rows_in[spot(source), :]

    def project(first, sources, weight, dest, part=None):
        many = len(sources) * CAP
        width = HD if many <= 384 and part is None else HALF

        def body(cols):
            w = weight[:, :, cols].reshape(D, width)
            result = jnp.dot(xs[first : first + many, :], w, preferred_element_type=F32).astype(BF16)
            for n, source in enumerate(sources):
                dest[spot(source), cols] = result[n * CAP : (n + 1) * CAP]

        if part is None:
            tiles(HD, width, body)
        else:
            body(pl.ds(part * HALF, HALF))

    causal = lax.broadcasted_iota(jnp.int32, (BLOCK, BLOCK), 0) >= lax.broadcasted_iota(
        jnp.int32, (BLOCK, BLOCK), 1
    )
    first_block = lax.rem((z + 1) // 2 + 3, 4)
    turn = [lax.rem(first_block + n, 4) for n in range(4)]

    def head_cols(h):
        return pl.ds(pl.multiple_of(h * DK, DK), DK)

    def state_rows(h):
        return pl.ds(pl.multiple_of((lax.rem(h, 2) * (HEADS // 2) + h // 2) * DK, DK), DK)

    def attend(blocks, h):
        cols = head_cols(h)
        for b in blocks:
            rows = pl.ds(pl.multiple_of(b * BLOCK, BLOCK), BLOCK)
            scores = lax.dot_general(
                q[rows, cols], k[rows, cols], (((1,), (1,)), ((), ())), preferred_element_type=F32
            )
            scores = jnp.where(causal, scores, 0.0).astype(BF16)
            reads[rows, cols] = jnp.dot(scores, v[rows, cols], preferred_element_type=F32)

    def add_up(blocks, h):
        cols = head_cols(h)
        for b in blocks:
            rows = pl.ds(pl.multiple_of(b * BLOCK, BLOCK), BLOCK)
            block_states[b, state_rows(h), :] = lax.dot_general(
                k[rows, cols], v[rows, cols], (((0,), (0,)), ((), ())), preferred_element_type=F32
            )

    near = [me, other] + [mem(z + d, c) for d in (-1, 1) for c in (core, 1 - core)]
    take(0, near)
    project(0, near, wk, k)
    arrive(asked, 12, 13)
    start(asked, 18, 19)
    project(0, near, wv, v)
    arrive(asked, 6, 7, 14, 15, 16, 17, 18, 19)
    halves = wq.at[:, pl.ds(half, CAP), :]
    swap = go(rcopy(halves, halves, swap_sems.at[0], swap_sems.at[1], {"mem": other}))
    middle = [mem(z + d, c) for d in (-2, 2) for c in (0, 1)]
    await_rows([mem(z + d, 1 - core) for d in (-2, 2)])
    take(384, middle)
    project(384, middle, wk, k)
    project(384, middle, wv, v)

    @pl.loop(0, HEADS)
    def _(h):
        add_up(turn[:2], h)

    far = [mem(z + d, c) for d in (-3, 3) for c in (0, 1)]
    swap.wait_recv()
    project(0, near + middle, wq, q)

    @pl.loop(0, 2)
    def _(h):
        attend(turn[:2], h)

    await_rows(far)
    take(640, far)
    project(640, far, wk, k)
    project(640, far, wv, v)
    last_ones = [mem(z + 4, c) for c in (0, 1)]
    await_rows(last_ones)
    take(896, last_ones)

    def at(row, column):
        return row * SIDE + column

    y1, y3 = y + 1 - 2 * (y % 2), SIDE - 1 - y
    x1, x3 = x + 1 - 2 * (x % 2), SIDE - 1 - x
    sums = [(at(y, x1), x % 2), (at(y, x3), x // 2), (at(y1, x), y % 2), (at(y3, x), y // 2)]
    befores = [(at(y3, x), 1 - y // 2), (at(y1, x), 1 - y % 2), (at(y, x3), 1 - x // 2), (at(y, x1), 1 - x % 2)]
    entering[...] = jnp.zeros_like(entering)
    moving = {}

    def low_high(pair):
        return pl.ds(pair * DK, DK), pl.ds(HALF + pair * DK, DK)

    def push(step, pair):
        low, high = low_high(pair)
        s_send[step, low, :] = total[low, :].astype(BF16)
        s_send[step, high, :] = (entering[high, :] + total[high, :] * befores[step][1].astype(F32)).astype(BF16)
        for stream, (rows, to) in enumerate(((low, sums[step][0]), (high, befores[step][0]))):
            sems = state_sems.at[step, pair, stream]
            src, dst = s_send.at[step, rows], s_recv.at[step, rows]
            moving[step, pair, stream] = go(rcopy(src, dst, sems.at[0], sems.at[1], {"seq": to}))

    def pull(step, pair):
        low, high = low_high(pair)
        moving[step, pair, 0].wait_recv()
        moving[step, pair, 1].wait_recv()
        theirs = s_recv[step, low, :].astype(F32)
        entering[low, :] += theirs * sums[step][1].astype(F32)
        if step < 3:
            total[low, :] += theirs
        entering[high, :] += s_recv[step, high, :].astype(F32)

    for pair in range(PARTS):
        if pair % 2 == 0:
            project(896, last_ones, wk, k, pair // 2)
            project(896, last_ones, wv, v, pair // 2)
        for h in (2 * pair, 2 * pair + 1):
            add_up(turn[2:], h)
        for rows in low_high(pair):
            total[rows, :] = (block_states[0, rows, :] + block_states[1, rows, :]) + (
                block_states[2, rows, :] + block_states[3, rows, :]
            )
        push(0, pair)
    project(640, far + last_ones, wq, q)
    running = jnp.zeros((HD, DK), F32)
    for b in range(4):
        before[b] = running.astype(BF16)
        running = running + block_states[b]
    tasks = [(turn[2:], h) for h in range(HEADS)] + [(turn[:2], h) for h in range(2, HEADS)]
    for step in range(3):
        for pair in range(PARTS):
            for task in tasks[step * PARTS + pair :: 3 * PARTS]:
                attend(*task)
            pull(step, pair)
            push(step + 1, pair)

    def finish(chip, part):
        chip = lax.rem(chip + RING, RING)
        rows = pl.ds(pl.multiple_of(chip * 128, 128), 128)
        for h in (2 * part, 2 * part + 1):
            cols = slice(h * DK, (h + 1) * DK)
            place = h % 2 * (HEADS // 2) + h // 2
            states = slice(place * DK, (place + 1) * DK)
            state = (entering[states, :] + before[chip // 2, states, :].astype(F32)).astype(BF16)
            read = reads[rows, cols] + jnp.dot(q[rows, cols], state, preferred_element_type=F32)
            scale = lax.rsqrt(jnp.mean(read * read, axis=1, keepdims=True) + 1e-6)
            normed[part, rows, h % 2 * DK : (h % 2 + 1) * DK] = (read * scale).astype(BF16)

    def give(part, source, node, side, number, sem):
        src, dst = normed.at[part, spot(source)], ret.at[side, part, spot(number)]
        go(rcopy(src, dst, ret_send.at[sem, part], ret_recv.at[side, number, part], {"mem": node}))

    back = []
    for part in range(PARTS):
        pull(3, part)
        finish(z + 4, part)
        for c in (0, 1):
            give(part, mem(z + 4, c), mem(z + 5 - 2 * core, c), core, 6, c)
        sem = 2
        for distance in (3, 2):
            for side in (0, 1):
                step = 1 - 2 * side
                finish(z - distance * step, part)
                for c in (0, 1):
                    source, node = mem(z - distance * step, c), mem(z - (distance - 1) * step, c)
                    give(part, source, node, side, 2 * (distance - 1) + core, sem)
                    sem += 1
        for side in (0, 1):
            chip = z - 1 + 2 * side
            finish(chip, part)
            give(part, mem(chip, 1 - core), other, side, 1, sem)
            sem += 1
            ret[side, part, 0:CAP, :] = normed[part, spot(mem(chip, core)), :]
        finish(z, part)
        src, dst = normed.at[part, spot(other)], own_ret.at[part, pl.ds(CAP, CAP), :]
        back.append(go(rcopy(src, dst, own_ret_sems.at[part, 0], own_ret_sems.at[part, 1], {"mem": other})))
        own_ret[part, 0:CAP, :] = normed[part, spot(me), :]

    parts = []
    for part in range(PARTS):
        for side in (0, 1):
            for number in range(1, 7):
                there = ret.at[side, part, pl.ds(number * CAP, CAP), :]
                sems = (ret_send.at[0, 0], ret_recv.at[side, number, part])
                rcopy(there, there, *sems, {"mem": other}).wait_recv()
            rows = ret[side, part]
            result = jnp.dot(gates[side, 0], rows, preferred_element_type=F32)
            result = result + jnp.dot(gates[side, 1], rows, preferred_element_type=F32)
            part_out[side, part] = result.astype(BF16)
            to = {"mem": mem(z - 1 + 2 * side, core)}
            src, dst, sems = part_out.at[side, part], part_in.at[side, part], part_sems.at[side, part]
            parts.append(go(rcopy(src, dst, sems.at[0], sems.at[1], to)))
    for part in range(PARTS):
        back[part].wait_recv()
        rows = own_ret[part]
        result = jnp.dot(own_gates[0], rows, preferred_element_type=F32)
        result = result + jnp.dot(own_gates[1], rows, preferred_element_type=F32)
        for side in (0, 1):
            parts[2 * part + side].wait_recv()
        result = result + part_in[0, part].astype(F32) + part_in[1, part].astype(F32)
        out[:, part * PART : (part + 1) * PART] = result.astype(BF16)
    for copy in sent:
        copy.wait_send()


def on_device(hidden, routes, gate_levels, query_weight, key_weight, value_weight):
    dma = pltpu.SemaphoreType.DMA
    whole = pl.BlockSpec(memory_space=pl.ANY)
    near = pl.BlockSpec(memory_space=pltpu.VMEM)
    return pl.pallas_call(
        kernel,
        out_shape=jax.ShapeDtypeStruct((TOK, HD), BF16),
        in_specs=[whole, near, near, whole, whole, whole],
        out_specs=near,
        scratch_shapes=[
            pltpu.VMEM((5, TOK, D), BF16),
            pltpu.VMEM((5, 2 * MEMS, TOK), F32),
            pltpu.VMEM((ROWS, D), BF16),
            pltpu.VMEM((2, 2 * CAP, D), BF16),
            pltpu.VMEM((2, 5 * CAP, D), BF16),
            pltpu.VMEM((2 * CAP, D), BF16),
            pltpu.VMEM((16, 128, HD), BF16),
            pltpu.VMEM((16, 128, HD), BF16),
            pltpu.VMEM((16, 128, HD), BF16),
            pltpu.VMEM((ROWS, HD), BF16),
            pltpu.VMEM((ROWS, HD), BF16),
            pltpu.VMEM((ROWS, HD), BF16),
            pltpu.VMEM((ROWS, D), BF16),
            pltpu.VMEM((4, HD, DK), F32),
            pltpu.VMEM((HD, DK), F32),
            pltpu.VMEM((HD, DK), F32),
            pltpu.VMEM((4, HD, DK), BF16),
            pltpu.VMEM((4, HD, DK), BF16),
            pltpu.VMEM((4, HD, DK), BF16),
            pltpu.VMEM((ROWS, HD), F32),
            pltpu.VMEM((PARTS, ROWS, PART), BF16),
            pltpu.VMEM((2, PARTS, 8 * CAP, PART), BF16),
            pltpu.VMEM((PARTS, 2 * CAP, PART), BF16),
            pltpu.VMEM((2, 2, TOK, 8 * CAP), BF16),
            pltpu.VMEM((2, TOK, 2 * CAP), BF16),
            pltpu.VMEM((2, PARTS, TOK, PART), BF16),
            pltpu.VMEM((2, PARTS, TOK, PART), BF16),
            dma((3, 20)),
            dma((3, 20)),
            dma((2, 2, 2, 2)),
            dma((2, 2, 2)),
            dma((2, 2)),
            dma((2, 5, 2)),
            dma((MEMS, 2)),
            dma((2,)),
            dma((4,)),
            dma((2,)),
            dma((4, PARTS, 2, 2)),
            dma((12, PARTS)),
            dma((2, 7, PARTS)),
            dma((PARTS, 2)),
            dma((2, PARTS, 2)),
        ],
        compiler_params=pltpu.CompilerParams(
            collective_id=0, has_side_effects=True, vmem_limit_bytes=58 * 2**20
        ),
        name="memories",
    )(hidden, routes.T, gate_levels.T, query_weight, key_weight, value_weight)


def solution(mesh):
    return jax.shard_map(
        on_device,
        mesh=mesh,
        in_specs=(
            P(("seq", "mem"), None),
            P(("seq", "mem"), None),
            P(("seq", "mem"), None),
            P("seq", None),
            P("mem", "seq", None),
            P("mem", "seq", None),
        ),
        out_specs=P(("seq", "mem"), None),
        check_vma=False,
    )
```
